32 devices in a mesh: grp: 2 (over y), seq: 8 (over z, x), mdl: 2 (over core).
Axes of the slice: x: 2, y: 2, z: 4, core: 2. Of those that a mesh axis runs over, the one named last changes fastest.
Arguments:
- tokens_in: bfloat16 [64, 8192], P(('grp', 'seq'), 'mdl'), parts along dimension 0, may hold values from -180 to 180
- norm_gain: float32 [8192], P('mdl'), may hold values from 0.5 to 1.5
- in_proj: bfloat16 [8, 3, 1024, 8192], P('seq', None, None, 'mdl'), may hold values from -0.0625 to 0.0625
- short_taps: float32 [7, 3, 8192], P(None, None, 'seq'), may hold values from -2.5 to 2.5
- long_taps: float32 [512, 128], replicated, may hold values from -0.5 to 0.5
- skip_bias: float32 [8192], P('seq'), may hold values from -6 to 6
- out_proj: bfloat16 [8192, 2, 4096], P('seq', 'mdl'), may hold values from -0.0625 to 0.0625
Outputs:
- mixed: bfloat16 [64, 8192], P('grp', 'seq'), parts along dimension 0
The draws below stay inside these ranges and needn't reach their ends.
There are 2 independent parts, one for each index of `grp`. The reference program is written for one: setup_inputs(seed, part) draws one part's arguments, and reference() takes and returns one part's arrays. A program takes and returns all parts, laid end to end along the dimension named above; an argument that names none is the same for every part. Nothing has to cross between parts.
All inputs are finite; a program needn't handle non-finite values.
Results may differ from the reference program's by a relative error of at most 0.007.
Values may be sent and summed in bfloat16 or wider, within the bound.
No kernel may reach another device: no remote copies, remote signals or barrier semaphores. Data moves between devices by JAX's collectives and lax.ppermute only.
A program may use at most 320 MiB of HBM per device.

```python
import math
import jax
import jax.numpy as jnp
from jax import lax

D = 8192
GROUP_CH = 16
FL = 128
SK = 7
TOKENS = 32
CH = 512
HALF = 4096
GROUPS = 512
N_SEQ = 8


def draw_tokens_in(key, part):
    key_base = jax.random.fold_in(key, 11)
    key_one, key_two, key_three = jax.random.split(key_base, 3)
    col_scale = jnp.exp(jax.random.uniform(key_three, (D,), jnp.float32, math.log(0.3), math.log(3.0)))
    base_vals = jnp.clip(jax.random.normal(key_one, (TOKENS, D), jnp.float32), -6.0, 6.0)
    row_scale = jnp.exp(jax.random.uniform(key_two, (TOKENS,), jnp.float32, 0.0, math.log(10.0)))
    return (base_vals * row_scale[:, None] * col_scale[None, :]).astype(jnp.bfloat16)


def level_of(own_key, dims, pieces, least, largest):
    def one(axis_at, parts):
        draws = jax.random.uniform(jax.random.fold_in(jax.random.fold_in(own_key, 6), axis_at), (parts,), jnp.float32, least / len(pieces), largest / len(pieces))
        return jnp.repeat(jnp.exp(draws), dims[axis_at] // parts).reshape((-1,) + (1,) * (len(dims) - axis_at - 1))

    gain = one(*pieces[0])
    for cut in pieces[1:]:
        gain = gain * one(*cut)
    return gain


def scatter_about(rng, shape, scale, reach, cuts=(), held_as=jnp.bfloat16):
    level = level_of(rng, shape, cuts, -0.22, 0.18) if cuts else 1.0
    entries = jax.random.normal(rng, shape, jnp.float32) * scale * level
    return jnp.minimum(jnp.maximum(entries, -reach), reach).astype(held_as)


def setup_inputs(seed: int = 0, part: int = 0) -> dict:
    seeds = jax.random.split(jax.random.key(seed), 8)
    part_keys = jax.random.split(jax.random.fold_in(seeds[7], part), 8)
    tokens_in = draw_tokens_in(jax.random.fold_in(jax.random.fold_in(seeds[7], part), 71), part)
    norm_gain = jnp.clip(1.0 + 0.1 * jax.random.normal(seeds[1], (D,), jnp.float32), 0.5, 1.5)
    in_proj = scatter_about(seeds[2], (N_SEQ, 3, 2 * CH, D), D ** -0.5, 0.0625, ((0, 8), (3, 2)))
    short_taps = scatter_about(seeds[3], (SK, 3, D), 0.4, 2.5, ((2, 8),), jnp.float32)
    long_taps = scatter_about(seeds[4], (GROUPS, FL), 0.09, 0.5, (), jnp.float32)
    skip_bias = scatter_about(seeds[5], (D,), 1.0, 6.0, ((0, 8),), jnp.float32)
    out_proj = scatter_about(seeds[6], (D, 2, HALF), D ** -0.5, 0.0625, ((0, 8), (1, 2)))
    return dict(tokens_in=tokens_in, norm_gain=norm_gain, in_proj=in_proj, short_taps=short_taps, long_taps=long_taps, skip_bias=skip_bias, out_proj=out_proj)


EPSILON = 1e-06

def reference(tokens_in, norm_gain, in_proj, short_taps, long_taps, skip_bias, out_proj):
    values = tokens_in.astype(jnp.float32)
    mean_square = lax.optimization_barrier(jnp.mean(values * values, axis=1, keepdims=True))
    normed = (values * lax.rsqrt(mean_square + EPSILON) * norm_gain[None, :]).astype(jnp.bfloat16)
    weights_in = jnp.transpose(in_proj, (3, 1, 0, 2)).reshape(D, 3 * D)
    projected = jnp.dot(normed, weights_in, preferred_element_type=jnp.float32).reshape(TOKENS, 3, D)
    padded = jnp.pad(projected, ((SK - 1, 0), (0, 0), (0, 0)))
    features = jnp.zeros((TOKENS, 3, D), jnp.float32)
    for offset in range(SK):
        features = features + short_taps[offset][None, :, :] * padded[SK - 1 - offset:SK - 1 - offset + TOKENS]
    gated_prod = features[:, 1, :] * features[:, 2, :]
    channel_taps = jnp.repeat(long_taps, GROUP_CH, axis=0)
    mixed_long = skip_bias[None, :] * gated_prod
    shifted = jnp.pad(gated_prod, ((FL - 1, 0), (0, 0)))
    for offset in range(FL):
        mixed_long = mixed_long + channel_taps[:, offset][None, :] * shifted[FL - 1 - offset:FL - 1 - offset + TOKENS]
    gated_out = (features[:, 0, :] * mixed_long).astype(jnp.bfloat16)
    weights_out = jnp.transpose(out_proj.reshape(D, 2, N_SEQ, CH), (2, 1, 3, 0)).reshape(D, D)
    return jnp.dot(gated_out, weights_out, preferred_element_type=jnp.float32).astype(jnp.bfloat16)
```

```python
import jax
import jax.numpy as jnp
from jax import lax
from jax.experimental import pallas as pl
from jax.experimental.pallas import tpu as pltpu
from jax.sharding import PartitionSpec as P

EPSILON = 1e-06
F32 = jnp.float32
BF16 = jnp.bfloat16
VMEM = pl.BlockSpec(memory_space=pltpu.VMEM)
ANY = pl.BlockSpec(memory_space=pl.ANY)
MIB = 1 << 20
LANES = 128
ROWS = 8


def contract_last(left, right):
    return lax.dot_general(left, right, (((1,), (1,)), ((), ())), preferred_element_type=F32)


def cost(flops, nbytes):
    return pl.CostEstimate(flops=flops, bytes_accessed=nbytes, transcendentals=0)


def params(mib):
    return pltpu.CompilerParams(vmem_limit_bytes=mib * MIB)


def swap(x, bits):
    count = lax.axis_size("seq")
    return lax.ppermute(x, "seq", [(i, i ^ bits) for i in range(count)])


def gather_pieces(x):
    pair = jnp.concatenate([x, swap(x, 1)], axis=0)
    return [pair] + [swap(pair, bits) for bits in (2, 4, 6)]


def projection_partner_kernel(a_ref, b_ref, c_ref, d_ref, gain_ref, w_ref, out_ref, xg_ref):
    tokens = xg_ref.shape[0]
    chan = w_ref.shape[1] // 2
    me = lax.axis_index("seq")
    other = 1 - lax.axis_index("mdl")
    raw = jnp.concatenate([a_ref[...], b_ref[...], c_ref[...], d_ref[...]], axis=0)
    per = tokens // lax.axis_size("seq")
    row = lax.broadcasted_iota(jnp.int32, (tokens, tokens), 0)
    col = lax.broadcasted_iota(jnp.int32, (tokens, tokens), 1)
    order = ((row // per) ^ me == col // per) & (row % per == col % per)
    select = jnp.where(order, 1.0, 0.0).astype(BF16)
    values = jnp.dot(select, raw, preferred_element_type=F32)
    squares = jnp.sum(values * values, axis=1, keepdims=True)
    xg_ref[...] = (values * gain_ref[...]).astype(BF16)
    first = pl.multiple_of(other * chan, chan)
    for branch in range(3):
        out_ref[:, branch * chan : (branch + 1) * chan] = contract_last(
            xg_ref[...], w_ref[branch, pl.ds(first, chan), :]
        )
    out_ref[:, 3 * chan :] = jnp.broadcast_to(squares, (tokens, LANES))


def projection_own_kernel(xg_ref, w_ref, out_ref):
    chan = w_ref.shape[1] // 2
    first = pl.multiple_of(lax.axis_index("mdl") * chan, chan)
    for branch in range(3):
        out_ref[:, branch * chan : (branch + 1) * chan] = contract_last(
            xg_ref[...], w_ref[branch, pl.ds(first, chan), :]
        )


def project(pieces, gain, weights, tokens):
    chan = weights.shape[1] // 2
    half = weights.shape[2]
    partner, xg = pl.pallas_call(
        projection_partner_kernel,
        out_shape=(
            jax.ShapeDtypeStruct((tokens, 3 * chan + LANES), F32),
            jax.ShapeDtypeStruct((tokens, half), BF16),
        ),
        in_specs=[VMEM] * 6,
        out_specs=(VMEM, VMEM),
        compiler_params=params(8),
        cost_estimate=cost(2 * tokens * half * 3 * chan, 2 * half * 3 * chan),
        name="project_partner",
    )(*pieces, gain, weights)
    own = pl.pallas_call(
        projection_own_kernel,
        out_shape=jax.ShapeDtypeStruct((tokens, 3 * chan), F32),
        in_specs=[VMEM] * 2,
        out_specs=VMEM,
        compiler_params=params(8),
        cost_estimate=cost(2 * tokens * half * 3 * chan, 2 * half * 3 * chan),
        name="project_own",
    )(xg, weights)
    got = lax.ppermute(partner, "mdl", [(0, 1), (1, 0)])
    return own, got, partner


def taps_kernel(taps_ref, out_ref):
    groups = taps_ref.shape[0]
    reach, chan = out_ref.shape
    per_group = chan // groups
    grp = lax.broadcasted_iota(jnp.int32, (groups, chan), 0)
    ch = lax.broadcasted_iota(jnp.int32, (groups, chan), 1)
    spread = jnp.where(ch // per_group == grp, 1.0, 0.0)
    out_ref[...] = lax.dot_general(
        taps_ref[...],
        spread,
        (((0,), (0,)), ((), ())),
        preferred_element_type=F32,
        precision=lax.Precision.HIGHEST,
    )[:reach]


def delay(x, rows):
    if rows == 0:
        return x
    index = lax.broadcasted_iota(jnp.int32, x.shape, 0)
    return jnp.where(index >= rows, pltpu.roll(x, rows, axis=0), 0.0)


def mix_kernel(width, own_ref, got_ref, sent_ref, short_ref, bias_ref, taps_ref, out_ref):
    tokens, chan = out_ref.shape
    reach = taps_ref.shape[0]
    first = pl.multiple_of(lax.axis_index("mdl") * chan, chan)
    squares = sent_ref[:, 3 * chan : 3 * chan + 1] + got_ref[:, 3 * chan : 3 * chan + 1]
    scale = lax.rsqrt(squares / width + EPSILON)
    feats = []
    for branch in range(3):
        cut = slice(branch * chan, (branch + 1) * chan)
        total = (own_ref[:, cut] + got_ref[:, cut]) * scale
        feat = None
        for offset in range(short_ref.shape[0]):
            term = short_ref[offset, pl.ds(branch, 1), pl.ds(first, chan)] * delay(total, offset)
            feat = term if feat is None else feat + term
        feats.append(feat)
    gated = feats[1] * feats[2]
    mixed = bias_ref[:, pl.ds(first, chan)] * gated
    blocks = [mixed[b * ROWS : (b + 1) * ROWS] for b in range(tokens // ROWS)]
    for shift in range(ROWS):
        moved = delay(gated, shift)
        for lag in range(reach // ROWS):
            tap = taps_ref[pl.ds(lag * ROWS + shift, 1), :]
            for b in range(lag, tokens // ROWS):
                blocks[b] = blocks[b] + tap * moved[(b - lag) * ROWS : (b - lag + 1) * ROWS]
    out_ref[...] = (feats[0] * jnp.concatenate(blocks, axis=0)).astype(BF16)


def spread_taps(long_taps, first_channel, chan, width, tokens):
    group_width = width // long_taps.shape[0]
    groups = chan // group_width
    local = lax.dynamic_slice_in_dim(long_taps, first_channel // group_width, groups, 0)
    reach = min(tokens, long_taps.shape[1])
    return pl.pallas_call(
        taps_kernel,
        out_shape=jax.ShapeDtypeStruct((reach, chan), F32),
        in_specs=[VMEM],
        out_specs=VMEM,
        compiler_params=params(4),
        name="spread_taps",
    )(local)


def mix(own, got, sent, short_taps, bias, taps, width):
    tokens, chan = own.shape[0], own.shape[1] // 3
    return pl.pallas_call(
        lambda *refs: mix_kernel(width, *refs),
        out_shape=jax.ShapeDtypeStruct((tokens, chan), BF16),
        in_specs=[VMEM] * 6,
        out_specs=VMEM,
        compiler_params=params(8),
        name="mix",
    )(own, got, sent, short_taps, bias, taps)


def out_kernel(a_ref, b_ref, c_ref, d_ref, w_ref, out_ref):
    tokens = out_ref.shape[0]
    chan = a_ref.shape[1]
    me = lax.axis_index("seq")
    total = None
    for place, ref in enumerate((a_ref, b_ref, c_ref, d_ref)):
        for low in range(2):
            owner = me ^ (2 * place + low)
            cut = pl.ds(pl.multiple_of(owner * chan, chan), chan)
            term = contract_last(ref[low * tokens : (low + 1) * tokens, :], w_ref[:, cut])
            total = term if total is None else total + term
    out_ref[...] = total


def project_out(pieces, weights, tokens):
    return pl.pallas_call(
        out_kernel,
        out_shape=jax.ShapeDtypeStruct((tokens, weights.shape[0]), F32),
        in_specs=[VMEM] * 5,
        out_specs=VMEM,
        compiler_params=params(8),
        cost_estimate=cost(2 * tokens * weights.size, 2 * weights.size),
        name="project_out",
    )(*pieces, weights)


def per_device(tokens_in, norm_gain, in_proj, short_taps, long_taps, skip_bias, out_proj):
    own_tokens, half = tokens_in.shape
    width = 2 * half
    tokens = own_tokens * lax.axis_size("seq")
    chan = in_proj.shape[2] // 2
    weights_in = in_proj.reshape(3, 2 * chan, half)
    weights_out = out_proj.reshape(out_proj.shape[0], -1)
    first_channel = lax.axis_index("seq") * 2 * chan + lax.axis_index("mdl") * chan
    taps = spread_taps(long_taps, first_channel, chan, width, tokens)
    pieces = gather_pieces(tokens_in)
    own, got, sent = project(pieces, norm_gain[None, :], weights_in, tokens)
    gated = mix(own, got, sent, short_taps, skip_bias[None, :], taps, width)
    partial_out = project_out(gather_pieces(gated), weights_out, tokens)
    other = lax.ppermute(partial_out, "mdl", [(0, 1), (1, 0)])
    return (partial_out + other).astype(BF16)


def per_device_any(tokens_in, norm_gain, in_proj, short_taps, long_taps, skip_bias, out_proj):
    half = tokens_in.shape[1]
    width = 2 * half
    chan = in_proj.shape[2] // 2
    seq_index = lax.axis_index("seq")
    mdl_index = lax.axis_index("mdl")
    values = tokens_in.astype(F32)
    squares = lax.psum(jnp.sum(values * values, axis=1), "mdl")
    scale = lax.rsqrt(squares / width + EPSILON)
    normed = (values * scale[:, None] * norm_gain[None, :]).astype(BF16)
    part = contract_last(
        lax.all_gather(normed, "seq", axis=0, tiled=True), in_proj.reshape(-1, half)
    )
    tokens = part.shape[0]
    part = part.reshape(tokens, 3, 2, chan)
    summed = lax.psum_scatter(part, "mdl", scatter_dimension=2, tiled=True)
    summed = summed.reshape(tokens, 3, chan)
    short_local = lax.dynamic_slice_in_dim(short_taps, mdl_index * chan, chan, 2)
    bias_local = lax.dynamic_slice_in_dim(skip_bias, mdl_index * chan, chan, 0)
    short_count = short_local.shape[0]
    padded = jnp.pad(summed, ((short_count - 1, 0), (0, 0), (0, 0)))
    features = sum(
        short_local[i][None] * padded[short_count - 1 - i : short_count - 1 - i + tokens]
        for i in range(short_count)
    )
    gated = features[:, 1, :] * features[:, 2, :]
    group_width = width // long_taps.shape[0]
    groups = (seq_index * 2 * chan + mdl_index * chan + jnp.arange(chan)) // group_width
    taps = long_taps[groups].T
    reach = min(tokens, taps.shape[0])
    shifted = jnp.pad(gated, ((reach - 1, 0), (0, 0)))
    mixed = bias_local[None, :] * gated + sum(
        taps[i][None, :] * shifted[reach - 1 - i : reach - 1 - i + tokens] for i in range(reach)
    )
    gated_out = (features[:, 0, :] * mixed).astype(BF16)
    rows = out_proj.reshape(out_proj.shape[0], -1)
    folded = contract_last(lax.all_gather(gated_out, "seq", axis=1, tiled=True), rows)
    return lax.psum(folded, "mdl").astype(BF16)


def solution(mesh):
    seq = mesh.shape["seq"]
    in_specs = (
        P(("grp", "seq"), "mdl"),
        P("mdl"),
        P("seq", None, None, "mdl"),
        P(None, None, "seq"),
        P(),
        P("seq"),
        P("seq", "mdl", None),
    )
    body = per_device if seq == 8 and mesh.shape["mdl"] == 2 else per_device_any
    return jax.shard_map(
        body, mesh=mesh, in_specs=in_specs, out_specs=P("grp", "seq"), check_vma=False
    )
```

```python
import jax
import jax.numpy as jnp
from jax import lax
from jax.experimental import pallas as pl
from jax.experimental.pallas import tpu as pltpu
from jax.sharding import PartitionSpec as P

EPSILON = 1e-06
F32 = jnp.float32
BF16 = jnp.bfloat16
VMEM = pl.BlockSpec(memory_space=pltpu.VMEM)
ANY = pl.BlockSpec(memory_space=pl.ANY)
MIB = 1 << 20
LANES = 128
ROWS = 8


def contract_last(left, right):
    return lax.dot_general(left, right, (((1,), (1,)), ((), ())), preferred_element_type=F32)


def cost(flops, nbytes):
    return pl.CostEstimate(flops=flops, bytes_accessed=nbytes, transcendentals=0)


def params(mib):
    return pltpu.CompilerParams(vmem_limit_bytes=mib * MIB)


def swap(x, bits):
    count = lax.axis_size("seq")
    return lax.ppermute(x, "seq", [(i, i ^ bits) for i in range(count)])


def stack_kernel(*refs):
    parts = [ref[...].astype(F32) for ref in refs[:-1]]
    refs[-1][...] = jnp.concatenate(parts, axis=0).astype(refs[-1].dtype)


def stack(*parts):
    rows = sum(part.shape[0] for part in parts)
    return pl.pallas_call(
        stack_kernel,
        out_shape=jax.ShapeDtypeStruct((rows,) + parts[0].shape[1:], parts[0].dtype),
        in_specs=[VMEM] * len(parts),
        out_specs=VMEM,
        compiler_params=params(4),
        name="stack",
    )(*parts)


ORDER = (0, 1, 2, 3, 4, 5, 6, 7)


def gather_pieces(x, local):
    pair = stack(local, swap(x, 1))
    return [pair] + [swap(pair, bits) for bits in (2, 4, 6)]


def in_vmem(x):
    return pltpu.with_memory_space_constraint(x, pltpu.VMEM)


def in_hbm(x):
    return pltpu.with_memory_space_constraint(x, pltpu.HBM)


def rows_of(which, chan):
    mine = lax.axis_index("mdl")
    return pl.multiple_of((mine if which == "own" else 1 - mine) * chan, chan)


CUTS = 2
PRE = 1
MORE = 4
NEXT = 4


def chunk_copies(which, w_ref, out_ref, sems, first, count):
    rows = out_ref.shape[1]
    start = rows_of(which, rows * CUTS)
    return [
        pltpu.make_async_copy(
            w_ref.at[i // CUTS, pl.ds(start + i % CUTS * rows, rows)],
            out_ref.at[i - first],
            sems.at[i - first],
        )
        for i in range(first, first + count)
    ]


def start_all(copies):
    for copy in copies:
        copy.start()


def wait_all(copies):
    for copy in copies:
        copy.wait()


def prepare_kernel(x_ref, w_ref, taps_ref, local_ref, chunks_ref, spread_ref, group_taps, sems, small):
    chan = spread_ref.shape[1]
    groups = group_taps.shape[0]
    index = lax.axis_index("seq") * 2 + lax.axis_index("mdl")
    near = pl.ds(pl.multiple_of(index * groups, groups), groups)
    fetch = pltpu.make_async_copy(taps_ref.at[near], group_taps, small.at[0])
    move = pltpu.make_async_copy(x_ref, local_ref, small.at[1])
    copies = chunk_copies("partner", w_ref, chunks_ref, sems, 0, PRE)
    start_all([fetch, move] + copies)
    fetch.wait()
    grp = lax.broadcasted_iota(jnp.int32, (groups, chan), 0)
    ch = lax.broadcasted_iota(jnp.int32, (groups, chan), 1)
    spread = jnp.where(ch // (chan // groups) == grp, 1.0, 0.0)
    spread_ref[...] = lax.dot_general(
        group_taps[...],
        spread,
        (((0,), (0,)), ((), ())),
        preferred_element_type=F32,
        precision=lax.Precision.HIGHEST,
    )[: spread_ref.shape[0]]
    wait_all([move] + copies)


def prepare(x, weights, long_taps, tokens):
    chan, half = weights.shape[1] // 2, weights.shape[2]
    reach = min(tokens, long_taps.shape[1])
    groups = long_taps.shape[0] * chan // (2 * half)
    return pl.pallas_call(
        prepare_kernel,
        out_shape=(
            jax.ShapeDtypeStruct(x.shape, x.dtype),
            pltpu.VMEM((PRE, chan // CUTS, half), weights.dtype),
            jax.ShapeDtypeStruct((reach, chan), F32),
        ),
        in_specs=[ANY] * 3,
        out_specs=(VMEM,) * 3,
        scratch_shapes=[
            pltpu.VMEM((groups, long_taps.shape[1]), F32),
            pltpu.SemaphoreType.DMA((PRE,)),
            pltpu.SemaphoreType.DMA((2,)),
        ],
        compiler_params=params(4),
        cost_estimate=cost(0, 4 * PRE * chan // CUTS * half),
        name="prepare",
    )(in_hbm(x), weights, in_hbm(long_taps))


def load_kernel(w_ref, after_ref, out_ref, sems):
    copies = chunk_copies("partner", w_ref, out_ref, sems, PRE, MORE)
    start_all(copies)
    wait_all(copies)


def load_more(weights, after):
    rows, half = weights.shape[1] // 2 // CUTS, weights.shape[2]
    return pl.pallas_call(
        load_kernel,
        out_shape=pltpu.VMEM((MORE, rows, half), weights.dtype),
        in_specs=[ANY, ANY],
        out_specs=VMEM,
        scratch_shapes=[pltpu.SemaphoreType.DMA((MORE,))],
        compiler_params=params(4),
        cost_estimate=cost(0, 4 * MORE * rows * half),
        name="load_more",
    )(weights, after)


def ordered(pieces, order, tokens):
    raw = jnp.concatenate([piece[...].astype(F32) for piece in pieces], axis=0).astype(BF16)
    me = lax.axis_index("seq")
    per = tokens // len(order)
    row = lax.broadcasted_iota(jnp.int32, (tokens, tokens), 0)
    col = lax.broadcasted_iota(jnp.int32, (tokens, tokens), 1)
    place = col // per
    bits = jnp.zeros_like(place)
    for k, value in enumerate(order):
        bits = jnp.where(place == k, value, bits)
    hit = ((row // per) ^ me == bits) & (row % per == col % per)
    return jnp.dot(jnp.where(hit, 1.0, 0.0).astype(BF16), raw, preferred_element_type=F32)


def chunk_products(xg_ref, refs, out_ref, at):
    for ref in refs:
        for i in range(ref.shape[0]):
            out_ref[:, at : at + ref.shape[1]] = contract_last(xg_ref[...], ref[i])
            at += ref.shape[1]
    return at


def in_order(work):
    pl.when(lax.axis_index("mdl") >= 0)(work)


def partner_kernel(
    a_ref, b_ref, c_ref, d_ref, gain_ref, pre_ref, more_ref, w_ref,
    out_ref, xg_ref, next_ref, last_ref, sems,
):
    tokens = out_ref.shape[0]
    rows = last_ref.shape[1]
    last = chunk_copies("partner", w_ref, last_ref, sems.at[0], PRE + MORE, last_ref.shape[0])
    following = chunk_copies("own", w_ref, next_ref, sems.at[1], 0, NEXT)
    start_all(last + following)

    @in_order
    def _():
        values = ordered((a_ref, b_ref, c_ref, d_ref), ORDER, tokens)
        squares = jnp.sum(values * values, axis=1, keepdims=True)
        out_ref[:, -LANES:] = jnp.broadcast_to(squares, (tokens, LANES))
        xg_ref[...] = (values * gain_ref[...]).astype(BF16)
        chunk_products(xg_ref, (pre_ref, more_ref), out_ref, 0)

    wait_all(last)

    @in_order
    def _():
        chunk_products(xg_ref, (last_ref,), out_ref, (PRE + MORE) * rows)

    wait_all(following)


def own_kernel(xg_ref, next_ref, w_ref, out_ref, last_ref, sems):
    rows = last_ref.shape[1]
    copies = chunk_copies("own", w_ref, last_ref, sems, NEXT, last_ref.shape[0])
    start_all(copies)

    @in_order
    def _():
        chunk_products(xg_ref, (next_ref,), out_ref, 0)

    wait_all(copies)
    chunk_products(xg_ref, (last_ref,), out_ref, NEXT * rows)


def project(tokens_in, gain, weights, long_taps, tokens):
    chan = weights.shape[1] // 2
    half = weights.shape[2]
    rows = chan // CUTS
    weights = in_hbm(weights)
    local, pre, taps = prepare(tokens_in, weights, long_taps, tokens)
    pieces = gather_pieces(tokens_in, local)
    more = load_more(weights, pieces[0])
    work = cost(2 * tokens * chan * half * 3, 2 * chan * half * 3)
    partner, xg, following = pl.pallas_call(
        partner_kernel,
        out_shape=(
            jax.ShapeDtypeStruct((tokens, 3 * chan + LANES), F32),
            jax.ShapeDtypeStruct((tokens, half), BF16),
            pltpu.VMEM((NEXT, rows, half), weights.dtype),
        ),
        in_specs=[VMEM] * 7 + [ANY],
        out_specs=(VMEM,) * 3,
        scratch_shapes=[
            pltpu.VMEM((3 * CUTS - PRE - MORE, rows, half), weights.dtype),
            pltpu.SemaphoreType.DMA((2, 3 * CUTS)),
        ],
        compiler_params=params(8),
        cost_estimate=work,
        name="project_partner",
    )(*pieces, gain, in_vmem(pre), in_vmem(more), weights)
    got = lax.ppermute(partner, "mdl", [(0, 1), (1, 0)])
    own = pl.pallas_call(
        own_kernel,
        out_shape=jax.ShapeDtypeStruct((tokens, 3 * chan), F32),
        in_specs=[VMEM] * 2 + [ANY],
        out_specs=VMEM,
        scratch_shapes=[
            pltpu.VMEM((3 * CUTS - NEXT, rows, half), weights.dtype),
            pltpu.SemaphoreType.DMA((3 * CUTS,)),
        ],
        compiler_params=params(8),
        cost_estimate=work,
        name="project_own",
    )(xg, in_vmem(following), weights)
    return own, got, partner, taps


def delay(x, rows):
    if rows == 0:
        return x
    index = lax.broadcasted_iota(jnp.int32, x.shape, 0)
    return jnp.where(index >= rows, pltpu.roll(x, rows, axis=0), 0.0)


def mix_kernel(width, own_ref, got_ref, sent_ref, short_ref, bias_ref, taps_ref, out_ref):
    tokens, chan = out_ref.shape
    reach = taps_ref.shape[0]
    first = pl.multiple_of(lax.axis_index("mdl") * chan, chan)
    squares = sent_ref[:, 3 * chan : 3 * chan + 1] + got_ref[:, 3 * chan : 3 * chan + 1]
    scale = lax.rsqrt(squares / width + EPSILON)
    feats = []
    for branch in range(3):
        span = slice(branch * chan, (branch + 1) * chan)
        total = (own_ref[:, span] + got_ref[:, span]) * scale
        feat = None
        for offset in range(short_ref.shape[1]):
            term = short_ref[branch, pl.ds(offset, 1), pl.ds(first, chan)] * delay(total, offset)
            feat = term if feat is None else feat + term
        feats.append(feat)
    gated = feats[1] * feats[2]
    mixed = bias_ref[:, pl.ds(first, chan)] * gated
    blocks = [mixed[b * ROWS : (b + 1) * ROWS] for b in range(tokens // ROWS)]
    for shift in range(ROWS):
        moved = delay(gated, shift)
        for lag in range(reach // ROWS):
            tap = taps_ref[pl.ds(lag * ROWS + shift, 1), :]
            for b in range(lag, tokens // ROWS):
                blocks[b] = blocks[b] + tap * moved[(b - lag) * ROWS : (b - lag + 1) * ROWS]
    out_ref[...] = (feats[0] * jnp.concatenate(blocks, axis=0)).astype(BF16)


def mix(own, got, sent, short_taps, bias, taps, width):
    tokens, chan = own.shape[0], own.shape[1] // 3
    return pl.pallas_call(
        lambda *refs: mix_kernel(width, *refs),
        out_shape=jax.ShapeDtypeStruct((tokens, chan), BF16),
        in_specs=[VMEM] * 6,
        out_specs=VMEM,
        compiler_params=params(8),
        name="mix",
    )(own, got, sent, jnp.transpose(short_taps, (1, 0, 2)), bias, taps)


def out_kernel(first, piece_ref, w_ref, *refs):
    out_ref = refs[-1]
    tokens, chan = out_ref.shape[0], piece_ref.shape[1]
    total = refs[0][...] if len(refs) > 1 else None
    for k in range(piece_ref.shape[0] // tokens):
        owner = lax.axis_index("seq") ^ ORDER[first + k]
        span = pl.ds(pl.multiple_of(owner * chan, chan), chan)
        term = contract_last(piece_ref[k * tokens : (k + 1) * tokens, :], w_ref[:, span])
        total = term if total is None else total + term
    out_ref[...] = total


def add_kernel(a_ref, b_ref, out_ref):
    out_ref[...] = (a_ref[...] + b_ref[...]).astype(out_ref.dtype)


def project_out(pieces, weights, tokens):
    total, first = [], 0
    for piece in pieces:
        count = piece.shape[0] // tokens
        width = count * piece.shape[1]
        total = [
            pl.pallas_call(
                lambda *refs, first=first: out_kernel(first, *refs),
                out_shape=jax.ShapeDtypeStruct((tokens, weights.shape[0]), F32),
                in_specs=[VMEM] * (2 + len(total)),
                out_specs=VMEM,
                compiler_params=params(8),
                cost_estimate=cost(2 * tokens * weights.shape[0] * width, 2 * weights.shape[0] * width),
                name="project_out",
            )(piece, weights, *total)
        ]
        first += count
    return total[0]


def per_device(tokens_in, norm_gain, in_proj, short_taps, long_taps, skip_bias, out_proj):
    own_tokens, half = tokens_in.shape
    width = 2 * half
    tokens = own_tokens * lax.axis_size("seq")
    chan = in_proj.shape[2] // 2
    weights_in = in_proj.reshape(3, 2 * chan, half)
    weights_out = out_proj.reshape(out_proj.shape[0], -1)
    own, got, sent, taps = project(tokens_in, norm_gain[None, :], weights_in, long_taps, tokens)
    gated = mix(own, got, sent, short_taps, skip_bias[None, :], taps, width)
    partial_out = project_out(gather_pieces(gated, gated), weights_out, tokens)
    other = lax.ppermute(partial_out, "mdl", [(0, 1), (1, 0)])
    return pl.pallas_call(
        add_kernel,
        out_shape=jax.ShapeDtypeStruct(other.shape, BF16),
        in_specs=[VMEM] * 2,
        out_specs=VMEM,
        compiler_params=params(4),
        name="add",
    )(partial_out, other)


def per_device_any(tokens_in, norm_gain, in_proj, short_taps, long_taps, skip_bias, out_proj):
    half = tokens_in.shape[1]
    width = 2 * half
    chan = in_proj.shape[2] // 2
    seq_index = lax.axis_index("seq")
    mdl_index = lax.axis_index("mdl")
    values = tokens_in.astype(F32)
    squares = lax.psum(jnp.sum(values * values, axis=1), "mdl")
    scale = lax.rsqrt(squares / width + EPSILON)
    normed = (values * scale[:, None] * norm_gain[None, :]).astype(BF16)
    part = contract_last(
        lax.all_gather(normed, "seq", axis=0, tiled=True), in_proj.reshape(-1, half)
    )
    tokens = part.shape[0]
    part = part.reshape(tokens, 3, 2, chan)
    summed = lax.psum_scatter(part, "mdl", scatter_dimension=2, tiled=True)
    summed = summed.reshape(tokens, 3, chan)
    short_local = lax.dynamic_slice_in_dim(short_taps, mdl_index * chan, chan, 2)
    bias_local = lax.dynamic_slice_in_dim(skip_bias, mdl_index * chan, chan, 0)
    short_count = short_local.shape[0]
    padded = jnp.pad(summed, ((short_count - 1, 0), (0, 0), (0, 0)))
    features = sum(
        short_local[i][None] * padded[short_count - 1 - i : short_count - 1 - i + tokens]
        for i in range(short_count)
    )
    gated = features[:, 1, :] * features[:, 2, :]
    group_width = width // long_taps.shape[0]
    groups = (seq_index * 2 * chan + mdl_index * chan + jnp.arange(chan)) // group_width
    taps = long_taps[groups].T
    reach = min(tokens, taps.shape[0])
    shifted = jnp.pad(gated, ((reach - 1, 0), (0, 0)))
    mixed = bias_local[None, :] * gated + sum(
        taps[i][None, :] * shifted[reach - 1 - i : reach - 1 - i + tokens] for i in range(reach)
    )
    gated_out = (features[:, 0, :] * mixed).astype(BF16)
    rows = out_proj.reshape(out_proj.shape[0], -1)
    folded = contract_last(lax.all_gather(gated_out, "seq", axis=1, tiled=True), rows)
    return lax.psum(folded, "mdl").astype(BF16)


def solution(mesh):
    seq = mesh.shape["seq"]
    in_specs = (
        P(("grp", "seq"), "mdl"),
        P("mdl"),
        P("seq", None, None, "mdl"),
        P(None, None, "seq"),
        P(),
        P("seq"),
        P("seq", "mdl", None),
    )
    body = per_device if seq == 8 and mesh.shape["mdl"] == 2 else per_device_any
    return jax.shard_map(
        body, mesh=mesh, in_specs=in_specs, out_specs=P("grp", "seq"), check_vma=False
    )
```

```python
import functools

import jax
import jax.numpy as jnp
from jax import lax
from jax.experimental import pallas as pl
from jax.experimental.pallas import tpu as pltpu
from jax.sharding import PartitionSpec as P

EPSILON = 1e-06
F32 = jnp.float32
BF16 = jnp.bfloat16
VMEM = pl.BlockSpec(memory_space=pltpu.VMEM)
ANY = pl.BlockSpec(memory_space=pl.ANY)
MIB = 1 << 20
LANES = 128
ROWS = 8


def contract_last(left, right):
    return lax.dot_general(left, right, (((1,), (1,)), ((), ())), preferred_element_type=F32)


def cost(flops, nbytes):
    return pl.CostEstimate(flops=flops, bytes_accessed=nbytes, transcendentals=0)


def params(mib):
    return pltpu.CompilerParams(vmem_limit_bytes=mib * MIB)


def swap(x, bits):
    count = lax.axis_size("seq")
    return lax.ppermute(x, "seq", [(i, i ^ bits) for i in range(count)])


def stack_kernel(*refs):
    parts = [ref[...].astype(F32) for ref in refs[:-1]]
    refs[-1][...] = jnp.concatenate(parts, axis=0).astype(refs[-1].dtype)


def stack(*parts):
    rows = sum(part.shape[0] for part in parts)
    return pl.pallas_call(
        stack_kernel,
        out_shape=jax.ShapeDtypeStruct((rows,) + parts[0].shape[1:], parts[0].dtype),
        in_specs=[VMEM] * len(parts),
        out_specs=VMEM,
        compiler_params=params(4),
        name="stack",
    )(*parts)


ORDER = (0, 1, 6, 7, 4, 5, 2, 3)


def gather_pieces(x, local):
    pair = stack(local, swap(x, 1))
    far, mid, near = [swap(pair, bits) for bits in (6, 4, 2)]
    return [pair, far, mid, near]


def in_vmem(x):
    return pltpu.with_memory_space_constraint(x, pltpu.VMEM)


def in_hbm(x):
    return pltpu.with_memory_space_constraint(x, pltpu.HBM)


def rows_of(which, chan):
    mine = lax.axis_index("mdl")
    return pl.multiple_of((mine if which == "own" else 1 - mine) * chan, chan)


def prepare_kernel(x_ref, taps_ref, local_ref, spread_ref, group_taps, sems):
    chan = spread_ref.shape[1]
    groups = group_taps.shape[0]
    index = lax.axis_index("seq") * 2 + lax.axis_index("mdl")
    near = pl.ds(pl.multiple_of(index * groups, groups), groups)
    fetch = pltpu.make_async_copy(taps_ref.at[near], group_taps, sems.at[0])
    move = pltpu.make_async_copy(x_ref, local_ref, sems.at[1])
    fetch.start()
    move.start()
    fetch.wait()
    grp = lax.broadcasted_iota(jnp.int32, (groups, chan), 0)
    ch = lax.broadcasted_iota(jnp.int32, (groups, chan), 1)
    spread = jnp.where(ch // (chan // groups) == grp, 1.0, 0.0)
    spread_ref[...] = lax.dot_general(
        group_taps[...],
        spread,
        (((0,), (0,)), ((), ())),
        preferred_element_type=F32,
        precision=lax.Precision.HIGHEST,
    )[: spread_ref.shape[0]]
    move.wait()


def prepare(x, long_taps, tokens, chan):
    reach = min(tokens, long_taps.shape[1])
    groups = long_taps.shape[0] * chan // (2 * x.shape[1])
    return pl.pallas_call(
        prepare_kernel,
        out_shape=(
            jax.ShapeDtypeStruct(x.shape, x.dtype),
            jax.ShapeDtypeStruct((reach, chan), F32),
        ),
        in_specs=[ANY] * 2,
        out_specs=(VMEM,) * 2,
        scratch_shapes=[
            pltpu.VMEM((groups, long_taps.shape[1]), F32),
            pltpu.SemaphoreType.DMA((2,)),
        ],
        compiler_params=params(4),
        cost_estimate=cost(12 * 10**9, 4 * MIB),
        name="prepare",
    )(in_hbm(x), in_hbm(long_taps))


def ordered(pieces, order, tokens):
    raw = jnp.concatenate([piece[...].astype(F32) for piece in pieces], axis=0).astype(BF16)
    me = lax.axis_index("seq")
    per = tokens // len(order)
    row = lax.broadcasted_iota(jnp.int32, (tokens, tokens), 0)
    col = lax.broadcasted_iota(jnp.int32, (tokens, tokens), 1)
    place = col // per
    bits = jnp.zeros_like(place)
    for k, value in enumerate(order):
        bits = jnp.where(place == k, value, bits)
    hit = ((row // per) ^ me == bits) & (row % per == col % per)
    return jnp.dot(jnp.where(hit, 1.0, 0.0).astype(BF16), raw, preferred_element_type=F32)


def partner_kernel(
    a_ref, b_ref, c_ref, d_ref, gain_ref, w_ref, wo_ref, out_ref, xg_ref, load_ref, sem
):
    load = pltpu.make_async_copy(wo_ref.at[pl.ds(0, load_ref.shape[0])], load_ref, sem)
    load.start()
    tokens = out_ref.shape[0]
    chan = w_ref.shape[2] // 2
    values = ordered((a_ref, b_ref, c_ref, d_ref), ORDER, tokens)
    squares = jnp.sum(values * values, axis=1, keepdims=True)
    out_ref[:, 3 * chan :] = jnp.broadcast_to(squares, (tokens, LANES))
    xg_ref[...] = (values * gain_ref[...]).astype(BF16)
    first = rows_of("partner", chan)
    for p in range(3):
        out_ref[:, p * chan : (p + 1) * chan] = contract_last(
            xg_ref[...], w_ref[0, p, pl.ds(first, chan), :]
        )
    load.wait()


def own_kernel(xg_ref, w_ref, wo_ref, out_ref, load_ref, sem):
    rows = load_ref.shape[0]
    load = pltpu.make_async_copy(wo_ref.at[pl.ds(wo_ref.shape[0] - rows, rows)], load_ref, sem)
    load.start()
    chan = w_ref.shape[2] // 2
    first = rows_of("own", chan)
    for p in range(3):
        out_ref[:, p * chan : (p + 1) * chan] = contract_last(
            xg_ref[...], w_ref[0, p, pl.ds(first, chan), :]
        )
    load.wait()


def project(tokens_in, gain, weights, weights_out, long_taps, tokens):
    chan = weights.shape[2] // 2
    half = weights.shape[3]
    local, taps = prepare(tokens_in, long_taps, tokens, chan)
    pieces = gather_pieces(tokens_in, local)
    work = cost(2 * tokens * chan * half * 3, weights.size)
    rows = weights_out.shape[0] // 2
    half_out = pltpu.VMEM((rows, weights_out.shape[1]), weights_out.dtype)
    weights_out = in_hbm(weights_out)
    partner, xg, low = pl.pallas_call(
        partner_kernel,
        out_shape=(
            jax.ShapeDtypeStruct((tokens, 3 * chan + LANES), F32),
            jax.ShapeDtypeStruct((tokens, half), BF16),
            half_out,
        ),
        in_specs=[VMEM] * 6 + [ANY],
        out_specs=(VMEM,) * 3,
        scratch_shapes=[pltpu.SemaphoreType.DMA],
        compiler_params=params(8),
        cost_estimate=work,
        name="project_partner",
    )(*pieces, gain, weights, weights_out)
    got = lax.ppermute(partner, "mdl", [(0, 1), (1, 0)])
    own, high = pl.pallas_call(
        own_kernel,
        out_shape=(
            jax.ShapeDtypeStruct((tokens, 3 * chan), F32),
            half_out,
        ),
        in_specs=[VMEM] * 2 + [ANY],
        out_specs=(VMEM,) * 2,
        scratch_shapes=[pltpu.SemaphoreType.DMA],
        compiler_params=params(8),
        cost_estimate=work,
        name="project_own",
    )(xg, weights, weights_out)
    return own, got, partner, taps, (in_vmem(low), in_vmem(high))


def delay(x, rows):
    if rows == 0:
        return x
    index = lax.broadcasted_iota(jnp.int32, x.shape, 0)
    return jnp.where(index >= rows, pltpu.roll(x, rows, axis=0), 0.0)


def mix_kernel(width, own_ref, got_ref, sent_ref, short_ref, bias_ref, taps_ref, out_ref):
    tokens, chan = out_ref.shape
    reach = taps_ref.shape[0]
    first = pl.multiple_of(lax.axis_index("mdl") * chan, chan)
    squares = sent_ref[:, 3 * chan : 3 * chan + 1] + got_ref[:, 3 * chan : 3 * chan + 1]
    scale = lax.rsqrt(squares / width + EPSILON)
    feats = []
    for branch in range(3):
        span = slice(branch * chan, (branch + 1) * chan)
        total = (own_ref[:, span] + got_ref[:, span]) * scale
        feat = None
        for offset in range(short_ref.shape[1]):
            term = short_ref[branch, pl.ds(offset, 1), pl.ds(first, chan)] * delay(total, offset)
            feat = term if feat is None else feat + term
        feats.append(feat)
    gated = feats[1] * feats[2]
    mixed = bias_ref[:, pl.ds(first, chan)] * gated
    blocks = [mixed[b * ROWS : (b + 1) * ROWS] for b in range(tokens // ROWS)]
    for shift in range(ROWS):
        moved = delay(gated, shift)
        for lag in range(reach // ROWS):
            tap = taps_ref[pl.ds(lag * ROWS + shift, 1), :]
            for b in range(lag, tokens // ROWS):
                blocks[b] = blocks[b] + tap * moved[(b - lag) * ROWS : (b - lag + 1) * ROWS]
    out_ref[...] = (feats[0] * jnp.concatenate(blocks, axis=0)).astype(BF16)


def mix(own, got, sent, short_taps, bias, taps, width):
    tokens, chan = own.shape[0], own.shape[1] // 3
    return pl.pallas_call(
        lambda *refs: mix_kernel(width, *refs),
        out_shape=jax.ShapeDtypeStruct((tokens, chan), BF16),
        in_specs=[VMEM] * 6,
        out_specs=VMEM,
        compiler_params=params(8),
        name="mix",
    )(own, got, sent, jnp.transpose(short_taps, (1, 0, 2)), bias, taps)


def out_kernel(piece_ref, low_ref, high_ref, *refs, first):
    out_ref = refs[-1]
    tokens, chan = out_ref.shape[0], piece_ref.shape[1]
    rows = low_ref.shape[0]
    for at, w_ref in ((0, low_ref), (rows, high_ref)):
        total = refs[0][:, at : at + rows] if len(refs) > 1 else None
        for k in range(piece_ref.shape[0] // tokens):
            owner = lax.axis_index("seq") ^ ORDER[first + k]
            span = pl.ds(pl.multiple_of(owner * chan, chan), chan)
            term = contract_last(piece_ref[k * tokens : (k + 1) * tokens, :], w_ref[:, span])
            total = term if total is None else total + term
        out_ref[:, at : at + rows] = total


def add_kernel(a_ref, b_ref, out_ref):
    out_ref[...] = (a_ref[...] + b_ref[...]).astype(out_ref.dtype)


def project_out(gated, low, high):
    tokens, rows = gated.shape[0], low.shape[0]
    pieces = gather_pieces(gated, gated)
    total, first = [], 0
    for piece in pieces:
        count = piece.shape[0] // tokens
        work = 2 * rows * count * piece.shape[1]
        total = [
            pl.pallas_call(
                functools.partial(out_kernel, first=first),
                out_shape=jax.ShapeDtypeStruct((tokens, 2 * rows), F32),
                in_specs=[VMEM] * (3 + len(total)),
                out_specs=VMEM,
                compiler_params=params(8),
                cost_estimate=cost(2 * tokens * work, 2 * work),
                name="project_out",
            )(piece, low, high, *total)
        ]
        first += count
    return total[0]


def per_device(tokens_in, norm_gain, in_proj, short_taps, long_taps, skip_bias, out_proj):
    own_tokens, half = tokens_in.shape
    width = 2 * half
    tokens = own_tokens * lax.axis_size("seq")
    chan = in_proj.shape[2] // 2
    weights_out = out_proj.reshape(out_proj.shape[0], -1)
    own, got, sent, taps, loaded = project(
        tokens_in, norm_gain[None, :], in_proj, weights_out, long_taps, tokens
    )
    gated = mix(own, got, sent, short_taps, skip_bias[None, :], taps, width)
    partial_out = project_out(gated, *loaded)
    other = lax.ppermute(partial_out, "mdl", [(0, 1), (1, 0)])
    return pl.pallas_call(
        add_kernel,
        out_shape=jax.ShapeDtypeStruct(other.shape, BF16),
        in_specs=[VMEM] * 2,
        out_specs=VMEM,
        compiler_params=params(4),
        name="add",
    )(partial_out, other)


def per_device_any(tokens_in, norm_gain, in_proj, short_taps, long_taps, skip_bias, out_proj):
    half = tokens_in.shape[1]
    width = 2 * half
    chan = in_proj.shape[2] // 2
    seq_index = lax.axis_index("seq")
    mdl_index = lax.axis_index("mdl")
    values = tokens_in.astype(F32)
    squares = lax.psum(jnp.sum(values * values, axis=1), "mdl")
    scale = lax.rsqrt(squares / width + EPSILON)
    normed = (values * scale[:, None] * norm_gain[None, :]).astype(BF16)
    part = contract_last(
        lax.all_gather(normed, "seq", axis=0, tiled=True), in_proj.reshape(-1, half)
    )
    tokens = part.shape[0]
    part = part.reshape(tokens, 3, 2, chan)
    summed = lax.psum_scatter(part, "mdl", scatter_dimension=2, tiled=True)
    summed = summed.reshape(tokens, 3, chan)
    short_local = lax.dynamic_slice_in_dim(short_taps, mdl_index * chan, chan, 2)
    bias_local = lax.dynamic_slice_in_dim(skip_bias, mdl_index * chan, chan, 0)
    short_count = short_local.shape[0]
    padded = jnp.pad(summed, ((short_count - 1, 0), (0, 0), (0, 0)))
    features = sum(
        short_local[i][None] * padded[short_count - 1 - i : short_count - 1 - i + tokens]
        for i in range(short_count)
    )
    gated = features[:, 1, :] * features[:, 2, :]
    group_width = width // long_taps.shape[0]
    groups = (seq_index * 2 * chan + mdl_index * chan + jnp.arange(chan)) // group_width
    taps = long_taps[groups].T
    reach = min(tokens, taps.shape[0])
    shifted = jnp.pad(gated, ((reach - 1, 0), (0, 0)))
    mixed = bias_local[None, :] * gated + sum(
        taps[i][None, :] * shifted[reach - 1 - i : reach - 1 - i + tokens] for i in range(reach)
    )
    gated_out = (features[:, 0, :] * mixed).astype(BF16)
    rows = out_proj.reshape(out_proj.shape[0], -1)
    folded = contract_last(lax.all_gather(gated_out, "seq", axis=1, tiled=True), rows)
    return lax.psum(folded, "mdl").astype(BF16)


def solution(mesh):
    seq = mesh.shape["seq"]
    in_specs = (
        P(("grp", "seq"), "mdl"),
        P("mdl"),
        P("seq", None, None, "mdl"),
        P(None, None, "seq"),
        P(),
        P("seq"),
        P("seq", "mdl", None),
    )
    body = per_device if seq == 8 and mesh.shape["mdl"] == 2 else per_device_any
    return jax.shard_map(
        body, mesh=mesh, in_specs=in_specs, out_specs=P("grp", "seq"), check_vma=False
    )
```

```python
import functools

import jax
import jax.numpy as jnp
from jax import lax
from jax.experimental import pallas as pl
from jax.experimental.pallas import tpu as pltpu
from jax.sharding import PartitionSpec as P

EPSILON = 1e-06
F32 = jnp.float32
BF16 = jnp.bfloat16
VMEM = pl.BlockSpec(memory_space=pltpu.VMEM)
ANY = pl.BlockSpec(memory_space=pl.ANY)
MIB = 1 << 20
LANES = 128
ROWS = 8


def contract_last(left, right):
    return lax.dot_general(left, right, (((1,), (1,)), ((), ())), preferred_element_type=F32)


def cost(flops, nbytes):
    return pl.CostEstimate(flops=flops, bytes_accessed=nbytes, transcendentals=0)


def params(mib):
    return pltpu.CompilerParams(vmem_limit_bytes=mib * MIB)


def swap(x, bits):
    count = lax.axis_size("seq")
    return lax.ppermute(x, "seq", [(i, i ^ bits) for i in range(count)])


def stack_kernel(*refs):
    parts = [ref[...].astype(F32) for ref in refs[:-1]]
    refs[-1][...] = jnp.concatenate(parts, axis=0).astype(refs[-1].dtype)


def stack(*parts):
    rows = sum(part.shape[0] for part in parts)
    return pl.pallas_call(
        stack_kernel,
        out_shape=jax.ShapeDtypeStruct((rows,) + parts[0].shape[1:], parts[0].dtype),
        in_specs=[VMEM] * len(parts),
        out_specs=VMEM,
        compiler_params=params(4),
        name="stack",
    )(*parts)


def gather_tokens(x, local):
    pair = stack(local, swap(x, 1))
    return [pair] + [swap(pair, b) for b in (6, 4, 2)], (0, 1, 6, 7, 4, 5, 2, 3)


def gather_groups(x):
    far, mid, close = [swap(x, b) for b in (6, 4, 2)]
    one, two = stack(x, far), stack(mid, close)
    return [([one, two], (0, 6, 4, 2)), ([swap(one, 1)], (1, 7)), ([swap(two, 1)], (5, 3))]


def in_vmem(x):
    return pltpu.with_memory_space_constraint(x, pltpu.VMEM)


def in_hbm(x):
    return pltpu.with_memory_space_constraint(x, pltpu.HBM)


def rows_of(which, chan):
    mine = lax.axis_index("mdl")
    return pl.multiple_of((mine if which == "own" else 1 - mine) * chan, chan)


def prepare_kernel(x_ref, taps_ref, local_ref, spread_ref, group_taps, sems):
    chan = spread_ref.shape[1]
    groups = group_taps.shape[0]
    index = lax.axis_index("seq") * 2 + lax.axis_index("mdl")
    near = pl.ds(pl.multiple_of(index * groups, groups), groups)
    fetch = pltpu.make_async_copy(taps_ref.at[near], group_taps, sems.at[0])
    move = pltpu.make_async_copy(x_ref, local_ref, sems.at[1])
    fetch.start()
    move.start()
    fetch.wait()
    grp = lax.broadcasted_iota(jnp.int32, (groups, chan), 0)
    ch = lax.broadcasted_iota(jnp.int32, (groups, chan), 1)
    spread = jnp.where(ch // (chan // groups) == grp, 1.0, 0.0)
    spread_ref[...] = lax.dot_general(
        group_taps[...],
        spread,
        (((0,), (0,)), ((), ())),
        preferred_element_type=F32,
        precision=lax.Precision.HIGHEST,
    )[: spread_ref.shape[0]]
    move.wait()


def prepare(x, long_taps, tokens, chan):
    reach = min(tokens, long_taps.shape[1])
    groups = long_taps.shape[0] * chan // (2 * x.shape[1])
    return pl.pallas_call(
        prepare_kernel,
        out_shape=(
            jax.ShapeDtypeStruct(x.shape, x.dtype),
            jax.ShapeDtypeStruct((reach, chan), F32),
        ),
        in_specs=[ANY] * 2,
        out_specs=(VMEM,) * 2,
        scratch_shapes=[
            pltpu.VMEM((groups, long_taps.shape[1]), F32),
            pltpu.SemaphoreType.DMA((2,)),
        ],
        compiler_params=params(4),
        cost_estimate=cost(12 * 10**9, 4 * MIB),
        name="prepare",
    )(in_hbm(x), in_hbm(long_taps))


def ordered(pieces, order, tokens):
    raw = jnp.concatenate([piece[...].astype(F32) for piece in pieces], axis=0).astype(BF16)
    me = lax.axis_index("seq")
    per = tokens // len(order)
    row = lax.broadcasted_iota(jnp.int32, (tokens, tokens), 0)
    col = lax.broadcasted_iota(jnp.int32, (tokens, tokens), 1)
    place = col // per
    bits = jnp.zeros_like(place)
    for k, value in enumerate(order):
        bits = jnp.where(place == k, value, bits)
    hit = ((row // per) ^ me == bits) & (row % per == col % per)
    return jnp.dot(jnp.where(hit, 1.0, 0.0).astype(BF16), raw, preferred_element_type=F32)


def partner_kernel(*refs, owners):
    pieces, (gain_ref, w_ref, wo_ref, out_ref, xg_ref, load_ref, sem) = refs[:-7], refs[-7:]
    load = pltpu.make_async_copy(wo_ref.at[pl.ds(0, load_ref.shape[0])], load_ref, sem)
    load.start()
    tokens = out_ref.shape[0]
    chan = w_ref.shape[2] // 2
    values = ordered(pieces, owners, tokens)
    squares = jnp.sum(values * values, axis=1, keepdims=True)
    out_ref[:, 3 * chan :] = jnp.broadcast_to(squares, (tokens, LANES))
    xg_ref[...] = (values * gain_ref[...]).astype(BF16)
    first = rows_of("partner", chan)
    for p in range(3):
        out_ref[:, p * chan : (p + 1) * chan] = contract_last(
            xg_ref[...], w_ref[0, p, pl.ds(first, chan), :]
        )
    load.wait()


def own_kernel(xg_ref, w_ref, wo_ref, out_ref, load_ref, sem):
    rows = load_ref.shape[0]
    load = pltpu.make_async_copy(wo_ref.at[pl.ds(wo_ref.shape[0] - rows, rows)], load_ref, sem)
    load.start()
    chan = w_ref.shape[2] // 2
    first = rows_of("own", chan)
    for p in range(3):
        out_ref[:, p * chan : (p + 1) * chan] = contract_last(
            xg_ref[...], w_ref[0, p, pl.ds(first, chan), :]
        )
    load.wait()


def project(tokens_in, gain, weights, weights_out, long_taps, tokens):
    chan = weights.shape[2] // 2
    half = weights.shape[3]
    local, taps = prepare(tokens_in, long_taps, tokens, chan)
    pieces, owners = gather_tokens(tokens_in, local)
    work = cost(2 * tokens * chan * half * 3, weights.size)
    rows = weights_out.shape[0] // 2
    half_out = pltpu.VMEM((rows, weights_out.shape[1]), weights_out.dtype)
    weights_out = in_hbm(weights_out)
    partner, xg, low = pl.pallas_call(
        functools.partial(partner_kernel, owners=owners),
        out_shape=(
            jax.ShapeDtypeStruct((tokens, 3 * chan + LANES), F32),
            jax.ShapeDtypeStruct((tokens, half), BF16),
            half_out,
        ),
        in_specs=[VMEM] * (2 + len(pieces)) + [ANY],
        out_specs=(VMEM,) * 3,
        scratch_shapes=[pltpu.SemaphoreType.DMA],
        compiler_params=params(8),
        cost_estimate=work,
        name="project_partner",
    )(*pieces, gain, weights, weights_out)
    got = lax.ppermute(partner, "mdl", [(0, 1), (1, 0)])
    own, high = pl.pallas_call(
        own_kernel,
        out_shape=(
            jax.ShapeDtypeStruct((tokens, 3 * chan), F32),
            half_out,
        ),
        in_specs=[VMEM] * 2 + [ANY],
        out_specs=(VMEM,) * 2,
        scratch_shapes=[pltpu.SemaphoreType.DMA],
        compiler_params=params(8),
        cost_estimate=work,
        name="project_own",
    )(xg, weights, weights_out)
    return own, got, partner, taps, (in_vmem(low), in_vmem(high))


def delay(x, rows):
    if rows == 0:
        return x
    index = lax.broadcasted_iota(jnp.int32, x.shape, 0)
    return jnp.where(index >= rows, pltpu.roll(x, rows, axis=0), 0.0)


def mix_kernel(width, own_ref, got_ref, sent_ref, short_ref, bias_ref, taps_ref, out_ref):
    tokens, chan = out_ref.shape
    reach = taps_ref.shape[0]
    first = pl.multiple_of(lax.axis_index("mdl") * chan, chan)
    squares = sent_ref[:, 3 * chan : 3 * chan + 1] + got_ref[:, 3 * chan : 3 * chan + 1]
    scale = lax.rsqrt(squares / width + EPSILON)
    feats = []
    for branch in range(3):
        span = slice(branch * chan, (branch + 1) * chan)
        total = (own_ref[:, span] + got_ref[:, span]) * scale
        feat = None
        for offset in range(short_ref.shape[1]):
            term = short_ref[branch, pl.ds(offset, 1), pl.ds(first, chan)] * delay(total, offset)
            feat = term if feat is None else feat + term
        feats.append(feat)
    gated = feats[1] * feats[2]
    mixed = bias_ref[:, pl.ds(first, chan)] * gated
    blocks = [mixed[b * ROWS : (b + 1) * ROWS] for b in range(tokens // ROWS)]
    for shift in range(ROWS):
        moved = delay(gated, shift)
        for lag in range(reach // ROWS):
            tap = taps_ref[pl.ds(lag * ROWS + shift, 1), :]
            for b in range(lag, tokens // ROWS):
                blocks[b] = blocks[b] + tap * moved[(b - lag) * ROWS : (b - lag + 1) * ROWS]
    out_ref[...] = (feats[0] * jnp.concatenate(blocks, axis=0)).astype(BF16)


def mix(own, got, sent, short_taps, bias, taps, width):
    tokens, chan = own.shape[0], own.shape[1] // 3
    return pl.pallas_call(
        lambda *refs: mix_kernel(width, *refs),
        out_shape=jax.ShapeDtypeStruct((tokens, chan), BF16),
        in_specs=[VMEM] * 6,
        out_specs=VMEM,
        compiler_params=params(8),
        name="mix",
    )(own, got, sent, jnp.transpose(short_taps, (1, 0, 2)), bias, taps)


def out_kernel(*refs, count, owners):
    pieces, (low_ref, high_ref, *acc, out_ref) = refs[:count], refs[count:]
    tokens, chan = out_ref.shape[0], pieces[0].shape[1]
    rows = low_ref.shape[0]
    shards = [ref[i : i + tokens, :] for ref in pieces for i in range(0, ref.shape[0], tokens)]
    for at, w_ref in ((0, low_ref), (rows, high_ref)):
        total = acc[0][:, at : at + rows] if acc else None
        for shard, bits in zip(shards, owners, strict=True):
            owner = lax.axis_index("seq") ^ bits
            span = pl.ds(pl.multiple_of(owner * chan, chan), chan)
            term = contract_last(shard, w_ref[:, span])
            total = term if total is None else total + term
        out_ref[:, at : at + rows] = total


def add_kernel(a_ref, b_ref, out_ref):
    out_ref[...] = (a_ref[...] + b_ref[...]).astype(out_ref.dtype)


def project_out(gated, low, high):
    tokens, rows = gated.shape[0], low.shape[0]
    total = []
    for pieces, owners in gather_groups(gated):
        work = 2 * rows * len(owners) * gated.shape[1]
        total = [
            pl.pallas_call(
                functools.partial(out_kernel, count=len(pieces), owners=owners),
                out_shape=jax.ShapeDtypeStruct((tokens, 2 * rows), F32),
                in_specs=[VMEM] * (len(pieces) + 2 + len(total)),
                out_specs=VMEM,
                compiler_params=params(8),
                cost_estimate=cost(2 * tokens * work, 2 * work),
                name="project_out",
            )(*pieces, low, high, *total)
        ]
    return total[0]


def per_device(tokens_in, norm_gain, in_proj, short_taps, long_taps, skip_bias, out_proj):
    own_tokens, half = tokens_in.shape
    width = 2 * half
    tokens = own_tokens * lax.axis_size("seq")
    chan = in_proj.shape[2] // 2
    weights_out = out_proj.reshape(out_proj.shape[0], -1)
    own, got, sent, taps, loaded = project(
        tokens_in, norm_gain[None, :], in_proj, weights_out, long_taps, tokens
    )
    gated = mix(own, got, sent, short_taps, skip_bias[None, :], taps, width)
    partial_out = project_out(gated, *loaded)
    other = lax.ppermute(partial_out, "mdl", [(0, 1), (1, 0)])
    return pl.pallas_call(
        add_kernel,
        out_shape=jax.ShapeDtypeStruct(other.shape, BF16),
        in_specs=[VMEM] * 2,
        out_specs=VMEM,
        compiler_params=params(4),
        name="add",
    )(partial_out, other)


def per_device_any(tokens_in, norm_gain, in_proj, short_taps, long_taps, skip_bias, out_proj):
    half = tokens_in.shape[1]
    width = 2 * half
    chan = in_proj.shape[2] // 2
    seq_index = lax.axis_index("seq")
    mdl_index = lax.axis_index("mdl")
    values = tokens_in.astype(F32)
    squares = lax.psum(jnp.sum(values * values, axis=1), "mdl")
    scale = lax.rsqrt(squares / width + EPSILON)
    normed = (values * scale[:, None] * norm_gain[None, :]).astype(BF16)
    part = contract_last(
        lax.all_gather(normed, "seq", axis=0, tiled=True), in_proj.reshape(-1, half)
    )
    tokens = part.shape[0]
    part = part.reshape(tokens, 3, 2, chan)
    summed = lax.psum_scatter(part, "mdl", scatter_dimension=2, tiled=True)
    summed = summed.reshape(tokens, 3, chan)
    short_local = lax.dynamic_slice_in_dim(short_taps, mdl_index * chan, chan, 2)
    bias_local = lax.dynamic_slice_in_dim(skip_bias, mdl_index * chan, chan, 0)
    short_count = short_local.shape[0]
    padded = jnp.pad(summed, ((short_count - 1, 0), (0, 0), (0, 0)))
    features = sum(
        short_local[i][None] * padded[short_count - 1 - i : short_count - 1 - i + tokens]
        for i in range(short_count)
    )
    gated = features[:, 1, :] * features[:, 2, :]
    group_width = width // long_taps.shape[0]
    groups = (seq_index * 2 * chan + mdl_index * chan + jnp.arange(chan)) // group_width
    taps = long_taps[groups].T
    reach = min(tokens, taps.shape[0])
    shifted = jnp.pad(gated, ((reach - 1, 0), (0, 0)))
    mixed = bias_local[None, :] * gated + sum(
        taps[i][None, :] * shifted[reach - 1 - i : reach - 1 - i + tokens] for i in range(reach)
    )
    gated_out = (features[:, 0, :] * mixed).astype(BF16)
    rows = out_proj.reshape(out_proj.shape[0], -1)
    folded = contract_last(lax.all_gather(gated_out, "seq", axis=1, tiled=True), rows)
    return lax.psum(folded, "mdl").astype(BF16)


def solution(mesh):
    seq = mesh.shape["seq"]
    in_specs = (
        P(("grp", "seq"), "mdl"),
        P("mdl"),
        P("seq", None, None, "mdl"),
        P(None, None, "seq"),
        P(),
        P("seq"),
        P("seq", "mdl", None),
    )
    body = per_device if seq == 8 and mesh.shape["mdl"] == 2 else per_device_any
    return jax.shard_map(
        body, mesh=mesh, in_specs=in_specs, out_specs=P("grp", "seq"), check_vma=False
    )
```

```python
import functools

import jax
import jax.numpy as jnp
from jax import lax
from jax.experimental import pallas as pl
from jax.experimental.pallas import tpu as pltpu
from jax.sharding import PartitionSpec as P

EPSILON = 1e-06
F32 = jnp.float32
BF16 = jnp.bfloat16
VMEM = pl.BlockSpec(memory_space=pltpu.VMEM)
ANY = pl.BlockSpec(memory_space=pl.ANY)
MIB = 1 << 20
LANES = 128
ROWS = 8


def contract_last(left, right):
    return lax.dot_general(left, right, (((1,), (1,)), ((), ())), preferred_element_type=F32)


def cost(flops, nbytes):
    return pl.CostEstimate(flops=flops, bytes_accessed=nbytes, transcendentals=0)


def params(mib):
    return pltpu.CompilerParams(vmem_limit_bytes=mib * MIB)


def swap(x, bits):
    count = lax.axis_size("seq")
    return lax.ppermute(x, "seq", [(i, i ^ bits) for i in range(count)])


def stack_kernel(*refs):
    parts = [ref[...].astype(F32) for ref in refs[:-1]]
    refs[-1][...] = jnp.concatenate(parts, axis=0).astype(refs[-1].dtype)


def stack(*parts):
    rows = sum(part.shape[0] for part in parts)
    return pl.pallas_call(
        stack_kernel,
        out_shape=jax.ShapeDtypeStruct((rows,) + parts[0].shape[1:], parts[0].dtype),
        in_specs=[VMEM] * len(parts),
        out_specs=VMEM,
        compiler_params=params(4),
        name="stack",
    )(*parts)


def gather_tokens(x, local):
    pair = stack(local, swap(x, 1))
    return [pair] + [swap(pair, b) for b in (6, 4, 2)], (0, 1, 6, 7, 4, 5, 2, 3)


def gather_groups(x):
    far, mid, close = [swap(x, b) for b in (6, 4, 2)]
    one, two = stack(x, far), stack(mid, close)
    return [([one, two], (0, 6, 4, 2)), ([swap(one, 1)], (1, 7)), ([swap(two, 1)], (5, 3))]


def in_vmem(x):
    return pltpu.with_memory_space_constraint(x, pltpu.VMEM)


def in_hbm(x):
    return pltpu.with_memory_space_constraint(x, pltpu.HBM)


def rows_of(which, chan):
    mine = lax.axis_index("mdl")
    return pl.multiple_of((mine if which == "own" else 1 - mine) * chan, chan)


def prepare_kernel(x_ref, taps_ref, local_ref, spread_ref, group_taps, sems):
    chan = spread_ref.shape[1]
    groups = group_taps.shape[0]
    index = lax.axis_index("seq") * 2 + lax.axis_index("mdl")
    near = pl.ds(pl.multiple_of(index * groups, groups), groups)
    fetch = pltpu.make_async_copy(taps_ref.at[near], group_taps, sems.at[0])
    move = pltpu.make_async_copy(x_ref, local_ref, sems.at[1])
    fetch.start()
    move.start()
    fetch.wait()
    grp = lax.broadcasted_iota(jnp.int32, (groups, chan), 0)
    ch = lax.broadcasted_iota(jnp.int32, (groups, chan), 1)
    spread = jnp.where(ch // (chan // groups) == grp, 1.0, 0.0)
    spread_ref[...] = lax.dot_general(
        group_taps[...],
        spread,
        (((0,), (0,)), ((), ())),
        preferred_element_type=F32,
        precision=lax.Precision.HIGHEST,
    )[: spread_ref.shape[0]]
    move.wait()


def prepare(x, long_taps, tokens, chan):
    reach = min(tokens, long_taps.shape[1])
    groups = long_taps.shape[0] * chan // (2 * x.shape[1])
    return pl.pallas_call(
        prepare_kernel,
        out_shape=(
            jax.ShapeDtypeStruct(x.shape, x.dtype),
            jax.ShapeDtypeStruct((reach, chan), F32),
        ),
        in_specs=[ANY] * 2,
        out_specs=(VMEM,) * 2,
        scratch_shapes=[
            pltpu.VMEM((groups, long_taps.shape[1]), F32),
            pltpu.SemaphoreType.DMA((2,)),
        ],
        compiler_params=params(4),
        cost_estimate=cost(12 * 10**9, 4 * MIB),
        name="prepare",
    )(in_hbm(x), in_hbm(long_taps))


def ordered(pieces, order, tokens):
    raw = jnp.concatenate([piece[...].astype(F32) for piece in pieces], axis=0).astype(BF16)
    me = lax.axis_index("seq")
    per = tokens // len(order)
    row = lax.broadcasted_iota(jnp.int32, (tokens, tokens), 0)
    col = lax.broadcasted_iota(jnp.int32, (tokens, tokens), 1)
    place = col // per
    bits = jnp.zeros_like(place)
    for k, value in enumerate(order):
        bits = jnp.where(place == k, value, bits)
    hit = ((row // per) ^ me == bits) & (row % per == col % per)
    return jnp.dot(jnp.where(hit, 1.0, 0.0).astype(BF16), raw, preferred_element_type=F32)


PUSH = 128
STREAM = 128
DEPTH = 512


def channel_sums(xg_ref, xt_ref, w_ref, which, out_ref, chan):
    tokens, half = xg_ref.shape
    first = rows_of(which, chan)
    for p in range(3):
        for at in range(0, chan, PUSH + STREAM):
            low = pl.ds(pl.multiple_of(first + at, PUSH), PUSH)
            high = pl.ds(pl.multiple_of(first + at + PUSH, STREAM), STREAM)
            pushed = streamed = None
            for depth in range(0, half, DEPTH):
                cut = slice(depth, depth + DEPTH)
                term = contract_last(xg_ref[:, cut], w_ref[0, p, low, cut])
                pushed = term if pushed is None else pushed + term
                term = jnp.dot(w_ref[0, p, high, cut], xt_ref[cut, :], preferred_element_type=F32)
                streamed = term if streamed is None else streamed + term
            to = p * chan + at
            out_ref[:, to : to + PUSH] = pushed
            out_ref[:, to + PUSH : to + PUSH + STREAM] = streamed.T


def partner_kernel(*refs, owners):
    pieces, refs = refs[:-8], refs[-8:]
    gain_ref, w_ref, wo_ref, out_ref, xg_ref, xt_ref, load_ref, sem = refs
    load = pltpu.make_async_copy(wo_ref.at[pl.ds(0, load_ref.shape[0])], load_ref, sem)
    load.start()
    tokens = out_ref.shape[0]
    values = ordered(pieces, owners, tokens)
    squares = jnp.sum(values * values, axis=1, keepdims=True)
    out_ref[:, -LANES:] = jnp.broadcast_to(squares, (tokens, LANES))
    gained = (values * gain_ref[...]).astype(BF16)
    xg_ref[...] = gained
    xt_ref[...] = gained.astype(F32).T.astype(BF16)
    channel_sums(xg_ref, xt_ref, w_ref, "partner", out_ref, w_ref.shape[2] // 2)
    load.wait()


def own_kernel(xg_ref, xt_ref, w_ref, wo_ref, out_ref, load_ref, sem):
    rows = load_ref.shape[0]
    load = pltpu.make_async_copy(wo_ref.at[pl.ds(wo_ref.shape[0] - rows, rows)], load_ref, sem)
    load.start()
    channel_sums(xg_ref, xt_ref, w_ref, "own", out_ref, w_ref.shape[2] // 2)
    load.wait()


def project(tokens_in, gain, weights, weights_out, long_taps, tokens):
    chan = weights.shape[2] // 2
    half = weights.shape[3]
    local, taps = prepare(tokens_in, long_taps, tokens, chan)
    pieces, owners = gather_tokens(tokens_in, local)
    work = cost(2 * tokens * chan * half * 3, weights.size)
    rows = weights_out.shape[0] // 2
    half_out = pltpu.VMEM((rows, weights_out.shape[1]), weights_out.dtype)
    weights_out = in_hbm(weights_out)
    partner, xg, xt, low = pl.pallas_call(
        functools.partial(partner_kernel, owners=owners),
        out_shape=(
            jax.ShapeDtypeStruct((tokens, 3 * chan + LANES), F32),
            jax.ShapeDtypeStruct((tokens, half), BF16),
            jax.ShapeDtypeStruct((half, tokens), BF16),
            half_out,
        ),
        in_specs=[VMEM] * (2 + len(pieces)) + [ANY],
        out_specs=(VMEM,) * 4,
        scratch_shapes=[pltpu.SemaphoreType.DMA],
        compiler_params=params(8),
        cost_estimate=work,
        name="project_partner",
    )(*pieces, gain, weights, weights_out)
    got = lax.ppermute(partner, "mdl", [(0, 1), (1, 0)])
    own, high = pl.pallas_call(
        own_kernel,
        out_shape=(
            jax.ShapeDtypeStruct((tokens, 3 * chan), F32),
            half_out,
        ),
        in_specs=[VMEM] * 3 + [ANY],
        out_specs=(VMEM,) * 2,
        scratch_shapes=[pltpu.SemaphoreType.DMA],
        compiler_params=params(8),
        cost_estimate=work,
        name="project_own",
    )(xg, xt, weights, weights_out)
    return own, got, partner, taps, (in_vmem(low), in_vmem(high))


def delay(x, rows):
    if rows == 0:
        return x
    index = lax.broadcasted_iota(jnp.int32, x.shape, 0)
    return jnp.where(index >= rows, pltpu.roll(x, rows, axis=0), 0.0)


def mix_kernel(width, own_ref, got_ref, sent_ref, short_ref, bias_ref, taps_ref, out_ref):
    tokens, chan = out_ref.shape
    reach = taps_ref.shape[0]
    first = pl.multiple_of(lax.axis_index("mdl") * chan, chan)
    squares = sent_ref[:, 3 * chan : 3 * chan + 1] + got_ref[:, 3 * chan : 3 * chan + 1]
    scale = lax.rsqrt(squares / width + EPSILON)
    feats = []
    for branch in range(3):
        span = slice(branch * chan, (branch + 1) * chan)
        total = (own_ref[:, span] + got_ref[:, span]) * scale
        feat = None
        for offset in range(short_ref.shape[1]):
            term = short_ref[branch, pl.ds(offset, 1), pl.ds(first, chan)] * delay(total, offset)
            feat = term if feat is None else feat + term
        feats.append(feat)
    gated = feats[1] * feats[2]
    mixed = bias_ref[:, pl.ds(first, chan)] * gated
    blocks = [mixed[b * ROWS : (b + 1) * ROWS] for b in range(tokens // ROWS)]
    for shift in range(ROWS):
        moved = delay(gated, shift)
        for lag in range(reach // ROWS):
            tap = taps_ref[pl.ds(lag * ROWS + shift, 1), :]
            for b in range(lag, tokens // ROWS):
                blocks[b] = blocks[b] + tap * moved[(b - lag) * ROWS : (b - lag + 1) * ROWS]
    out_ref[...] = (feats[0] * jnp.concatenate(blocks, axis=0)).astype(BF16)


def mix(own, got, sent, short_taps, bias, taps, width):
    tokens, chan = own.shape[0], own.shape[1] // 3
    return pl.pallas_call(
        lambda *refs: mix_kernel(width, *refs),
        out_shape=jax.ShapeDtypeStruct((tokens, chan), BF16),
        in_specs=[VMEM] * 6,
        out_specs=VMEM,
        compiler_params=params(8),
        name="mix",
    )(own, got, sent, jnp.transpose(short_taps, (1, 0, 2)), bias, taps)


def out_kernel(*refs, count, owners):
    pieces, (low_ref, high_ref, *acc, out_ref) = refs[:count], refs[count:]
    tokens, chan = out_ref.shape[0], pieces[0].shape[1]
    rows = low_ref.shape[0]
    shards = [ref[i : i + tokens, :] for ref in pieces for i in range(0, ref.shape[0], tokens)]
    for at, w_ref in ((0, low_ref), (rows, high_ref)):
        total = acc[0][:, at : at + rows] if acc else None
        for shard, bits in zip(shards, owners, strict=True):
            owner = lax.axis_index("seq") ^ bits
            span = pl.ds(pl.multiple_of(owner * chan, chan), chan)
            term = contract_last(shard, w_ref[:, span])
            total = term if total is None else total + term
        out_ref[:, at : at + rows] = total


def add_kernel(a_ref, b_ref, out_ref):
    out_ref[...] = (a_ref[...] + b_ref[...]).astype(out_ref.dtype)


def project_out(gated, low, high):
    tokens, rows = gated.shape[0], low.shape[0]
    total = []
    for pieces, owners in gather_groups(gated):
        work = 2 * rows * len(owners) * gated.shape[1]
        total = [
            pl.pallas_call(
                functools.partial(out_kernel, count=len(pieces), owners=owners),
                out_shape=jax.ShapeDtypeStruct((tokens, 2 * rows), F32),
                in_specs=[VMEM] * (len(pieces) + 2 + len(total)),
                out_specs=VMEM,
                compiler_params=params(8),
                cost_estimate=cost(2 * tokens * work, 2 * work),
                name="project_out",
            )(*pieces, low, high, *total)
        ]
    return total[0]


def per_device(tokens_in, norm_gain, in_proj, short_taps, long_taps, skip_bias, out_proj):
    own_tokens, half = tokens_in.shape
    width = 2 * half
    tokens = own_tokens * lax.axis_size("seq")
    chan = in_proj.shape[2] // 2
    weights_out = out_proj.reshape(out_proj.shape[0], -1)
    own, got, sent, taps, loaded = project(
        tokens_in, norm_gain[None, :], in_proj, weights_out, long_taps, tokens
    )
    gated = mix(own, got, sent, short_taps, skip_bias[None, :], taps, width)
    partial_out = project_out(gated, *loaded)
    other = lax.ppermute(partial_out, "mdl", [(0, 1), (1, 0)])
    return pl.pallas_call(
        add_kernel,
        out_shape=jax.ShapeDtypeStruct(other.shape, BF16),
        in_specs=[VMEM] * 2,
        out_specs=VMEM,
        compiler_params=params(4),
        name="add",
    )(partial_out, other)


def per_device_any(tokens_in, norm_gain, in_proj, short_taps, long_taps, skip_bias, out_proj):
    half = tokens_in.shape[1]
    width = 2 * half
    chan = in_proj.shape[2] // 2
    seq_index = lax.axis_index("seq")
    mdl_index = lax.axis_index("mdl")
    values = tokens_in.astype(F32)
    squares = lax.psum(jnp.sum(values * values, axis=1), "mdl")
    scale = lax.rsqrt(squares / width + EPSILON)
    normed = (values * scale[:, None] * norm_gain[None, :]).astype(BF16)
    part = contract_last(
        lax.all_gather(normed, "seq", axis=0, tiled=True), in_proj.reshape(-1, half)
    )
    tokens = part.shape[0]
    part = part.reshape(tokens, 3, 2, chan)
    summed = lax.psum_scatter(part, "mdl", scatter_dimension=2, tiled=True)
    summed = summed.reshape(tokens, 3, chan)
    short_local = lax.dynamic_slice_in_dim(short_taps, mdl_index * chan, chan, 2)
    bias_local = lax.dynamic_slice_in_dim(skip_bias, mdl_index * chan, chan, 0)
    short_count = short_local.shape[0]
    padded = jnp.pad(summed, ((short_count - 1, 0), (0, 0), (0, 0)))
    features = sum(
        short_local[i][None] * padded[short_count - 1 - i : short_count - 1 - i + tokens]
        for i in range(short_count)
    )
    gated = features[:, 1, :] * features[:, 2, :]
    group_width = width // long_taps.shape[0]
    groups = (seq_index * 2 * chan + mdl_index * chan + jnp.arange(chan)) // group_width
    taps = long_taps[groups].T
    reach = min(tokens, taps.shape[0])
    shifted = jnp.pad(gated, ((reach - 1, 0), (0, 0)))
    mixed = bias_local[None, :] * gated + sum(
        taps[i][None, :] * shifted[reach - 1 - i : reach - 1 - i + tokens] for i in range(reach)
    )
    gated_out = (features[:, 0, :] * mixed).astype(BF16)
    rows = out_proj.reshape(out_proj.shape[0], -1)
    folded = contract_last(lax.all_gather(gated_out, "seq", axis=1, tiled=True), rows)
    return lax.psum(folded, "mdl").astype(BF16)


def solution(mesh):
    seq = mesh.shape["seq"]
    in_specs = (
        P(("grp", "seq"), "mdl"),
        P("mdl"),
        P("seq", None, None, "mdl"),
        P(None, None, "seq"),
        P(),
        P("seq"),
        P("seq", "mdl", None),
    )

    def body(tokens_in, norm_gain, in_proj, *others):
        half, chan = tokens_in.shape[1], in_proj.shape[2] // 2
        fits = seq == 8 and mesh.shape["mdl"] == 2
        fits = fits and chan % (PUSH + STREAM) == 0 and half % DEPTH == 0
        path = per_device if fits else per_device_any
        return path(tokens_in, norm_gain, in_proj, *others)

    return jax.shard_map(
        body, mesh=mesh, in_specs=in_specs, out_specs=P("grp", "seq"), check_vma=False
    )
```

```python
import functools

import jax
import jax.numpy as jnp
from jax import lax
from jax.experimental import pallas as pl
from jax.experimental.pallas import tpu as pltpu
from jax.sharding import PartitionSpec as P

EPSILON = 1e-06
F32 = jnp.float32
BF16 = jnp.bfloat16
VMEM = pl.BlockSpec(memory_space=pltpu.VMEM)
ANY = pl.BlockSpec(memory_space=pl.ANY)
MIB = 1 << 20
LANES = 128
ROWS = 8


def contract_last(left, right):
    return lax.dot_general(left, right, (((1,), (1,)), ((), ())), preferred_element_type=F32)


def cost(flops, nbytes):
    return pl.CostEstimate(flops=flops, bytes_accessed=nbytes, transcendentals=0)


def params(mib):
    return pltpu.CompilerParams(vmem_limit_bytes=mib * MIB)


def swap(x, bits):
    count = lax.axis_size("seq")
    return lax.ppermute(x, "seq", [(i, i ^ bits) for i in range(count)])


def stack_kernel(*refs):
    parts = [ref[...].astype(F32) for ref in refs[:-1]]
    refs[-1][...] = jnp.concatenate(parts, axis=0).astype(refs[-1].dtype)


def stack(*parts):
    rows = sum(part.shape[0] for part in parts)
    return pl.pallas_call(
        stack_kernel,
        out_shape=jax.ShapeDtypeStruct((rows,) + parts[0].shape[1:], parts[0].dtype),
        in_specs=[VMEM] * len(parts),
        out_specs=VMEM,
        compiler_params=params(4),
        name="stack",
    )(*parts)


def gather_tokens(x, local):
    pair = stack(local, swap(x, 1))
    return [pair] + [swap(pair, b) for b in (6, 4, 2)], (0, 1, 6, 7, 4, 5, 2, 3)


def gather_groups(x):
    far, mid, close = [swap(x, b) for b in (6, 4, 2)]
    one, two = stack(x, far), stack(mid, close)
    return [([one, two], (0, 6, 4, 2)), ([swap(one, 1)], (1, 7)), ([swap(two, 1)], (5, 3))]


def in_vmem(x):
    return pltpu.with_memory_space_constraint(x, pltpu.VMEM)


def in_hbm(x):
    return pltpu.with_memory_space_constraint(x, pltpu.HBM)


def rows_of(which, chan):
    mine = lax.axis_index("mdl")
    return pl.multiple_of((mine if which == "own" else 1 - mine) * chan, chan)


def prepare_kernel(x_ref, taps_ref, local_ref, spread_ref, group_taps, sems):
    chan = spread_ref.shape[1]
    groups = group_taps.shape[0]
    index = lax.axis_index("seq") * 2 + lax.axis_index("mdl")
    near = pl.ds(pl.multiple_of(index * groups, groups), groups)
    fetch = pltpu.make_async_copy(taps_ref.at[near], group_taps, sems.at[0])
    move = pltpu.make_async_copy(x_ref, local_ref, sems.at[1])
    fetch.start()
    move.start()
    fetch.wait()
    grp = lax.broadcasted_iota(jnp.int32, (groups, chan), 0)
    ch = lax.broadcasted_iota(jnp.int32, (groups, chan), 1)
    spread = jnp.where(ch // (chan // groups) == grp, 1.0, 0.0)
    spread_ref[...] = lax.dot_general(
        group_taps[...],
        spread,
        (((0,), (0,)), ((), ())),
        preferred_element_type=F32,
        precision=lax.Precision.HIGHEST,
    )[: spread_ref.shape[0]]
    move.wait()


def prepare(x, long_taps, tokens, chan):
    reach = min(tokens, long_taps.shape[1])
    groups = long_taps.shape[0] * chan // (2 * x.shape[1])
    return pl.pallas_call(
        prepare_kernel,
        out_shape=(
            jax.ShapeDtypeStruct(x.shape, x.dtype),
            jax.ShapeDtypeStruct((reach, chan), F32),
        ),
        in_specs=[ANY] * 2,
        out_specs=(VMEM,) * 2,
        scratch_shapes=[
            pltpu.VMEM((groups, long_taps.shape[1]), F32),
            pltpu.SemaphoreType.DMA((2,)),
        ],
        compiler_params=params(4),
        cost_estimate=cost(12 * 10**9, 4 * MIB),
        name="prepare",
    )(in_hbm(x), in_hbm(long_taps))


def place_rows(pieces, owners, out_ref):
    per = out_ref.shape[1]
    shards = [
        piece[...].astype(F32)[i : i + per]
        for piece in pieces
        for i in range(0, piece.shape[0], per)
    ]
    for shard, bits in zip(shards, owners, strict=True):
        out_ref[lax.axis_index("seq") ^ bits] = shard


PUSH = 128
STREAM = 128
DEPTH = 512


def channel_sums(xg_ref, xt_ref, w_ref, which, out_ref, chan):
    tokens, half = xg_ref.shape
    first = rows_of(which, chan)
    for p in range(3):
        for at in range(0, chan, PUSH + STREAM):
            low = pl.ds(pl.multiple_of(first + at, PUSH), PUSH)
            high = pl.ds(pl.multiple_of(first + at + PUSH, STREAM), STREAM)
            pushed = streamed = None
            for depth in range(0, half, DEPTH):
                cut = slice(depth, depth + DEPTH)
                term = contract_last(xg_ref[:, cut], w_ref[0, p, low, cut])
                pushed = term if pushed is None else pushed + term
                term = jnp.dot(w_ref[0, p, high, cut], xt_ref[cut, :], preferred_element_type=F32)
                streamed = term if streamed is None else streamed + term
            to = p * chan + at
            out_ref[:, to : to + PUSH] = pushed
            out_ref[:, to + PUSH : to + PUSH + STREAM] = streamed.T


def partner_kernel(*refs, owners):
    pieces, refs = refs[:-9], refs[-9:]
    gain_ref, w_ref, wo_ref, out_ref, xg_ref, xt_ref, load_ref, raw_ref, sem = refs
    load = pltpu.make_async_copy(wo_ref.at[pl.ds(0, load_ref.shape[0])], load_ref, sem)
    load.start()
    tokens = out_ref.shape[0]
    place_rows(pieces, owners, raw_ref)
    values = jnp.concatenate([raw_ref[i] for i in range(raw_ref.shape[0])], axis=0)
    squares = jnp.sum(values * values, axis=1, keepdims=True)
    out_ref[:, -LANES:] = jnp.broadcast_to(squares, (tokens, LANES))
    gained = (values * gain_ref[...]).astype(BF16)
    xg_ref[...] = gained
    xt_ref[...] = gained.astype(F32).T.astype(BF16)
    channel_sums(xg_ref, xt_ref, w_ref, "partner", out_ref, w_ref.shape[2] // 2)
    load.wait()


def own_kernel(xg_ref, xt_ref, w_ref, wo_ref, out_ref, load_ref, sem):
    rows = load_ref.shape[0]
    load = pltpu.make_async_copy(wo_ref.at[pl.ds(wo_ref.shape[0] - rows, rows)], load_ref, sem)
    load.start()
    channel_sums(xg_ref, xt_ref, w_ref, "own", out_ref, w_ref.shape[2] // 2)
    load.wait()


def project(tokens_in, gain, weights, weights_out, long_taps, tokens):
    chan = weights.shape[2] // 2
    half = weights.shape[3]
    local, taps = prepare(tokens_in, long_taps, tokens, chan)
    pieces, owners = gather_tokens(tokens_in, local)
    work = cost(2 * tokens * chan * half * 3, weights.size)
    rows = weights_out.shape[0] // 2
    half_out = pltpu.VMEM((rows, weights_out.shape[1]), weights_out.dtype)
    weights_out = in_hbm(weights_out)
    partner, xg, xt, low = pl.pallas_call(
        functools.partial(partner_kernel, owners=owners),
        out_shape=(
            jax.ShapeDtypeStruct((tokens, 3 * chan + LANES), F32),
            jax.ShapeDtypeStruct((tokens, half), BF16),
            jax.ShapeDtypeStruct((half, tokens), BF16),
            half_out,
        ),
        in_specs=[VMEM] * (2 + len(pieces)) + [ANY],
        out_specs=(VMEM,) * 4,
        scratch_shapes=[
            pltpu.VMEM((len(owners), tokens // len(owners), half), F32),
            pltpu.SemaphoreType.DMA,
        ],
        compiler_params=params(8),
        cost_estimate=work,
        name="project_partner",
    )(*pieces, gain, weights, weights_out)
    got = lax.ppermute(partner, "mdl", [(0, 1), (1, 0)])
    own, high = pl.pallas_call(
        own_kernel,
        out_shape=(
            jax.ShapeDtypeStruct((tokens, 3 * chan), F32),
            half_out,
        ),
        in_specs=[VMEM] * 3 + [ANY],
        out_specs=(VMEM,) * 2,
        scratch_shapes=[pltpu.SemaphoreType.DMA],
        compiler_params=params(8),
        cost_estimate=work,
        name="project_own",
    )(xg, xt, weights, weights_out)
    return own, got, partner, taps, (in_vmem(low), in_vmem(high))


def delay(x, rows):
    if rows == 0:
        return x
    index = lax.broadcasted_iota(jnp.int32, x.shape, 0)
    return jnp.where(index >= rows, pltpu.roll(x, rows, axis=0), 0.0)


def mix_kernel(width, own_ref, got_ref, sent_ref, short_ref, bias_ref, taps_ref, out_ref):
    tokens, chan = out_ref.shape
    reach = taps_ref.shape[0]
    first = pl.multiple_of(lax.axis_index("mdl") * chan, chan)
    squares = sent_ref[:, 3 * chan : 3 * chan + 1] + got_ref[:, 3 * chan : 3 * chan + 1]
    scale = lax.rsqrt(squares / width + EPSILON)
    feats = []
    for branch in range(3):
        span = slice(branch * chan, (branch + 1) * chan)
        total = (own_ref[:, span] + got_ref[:, span]) * scale
        feat = None
        for offset in range(short_ref.shape[1]):
            term = short_ref[branch, pl.ds(offset, 1), pl.ds(first, chan)] * delay(total, offset)
            feat = term if feat is None else feat + term
        feats.append(feat)
    gated = feats[1] * feats[2]
    mixed = bias_ref[:, pl.ds(first, chan)] * gated
    blocks = [mixed[b * ROWS : (b + 1) * ROWS] for b in range(tokens // ROWS)]
    for shift in range(ROWS):
        moved = delay(gated, shift)
        for lag in range(reach // ROWS):
            tap = taps_ref[pl.ds(lag * ROWS + shift, 1), :]
            for b in range(lag, tokens // ROWS):
                blocks[b] = blocks[b] + tap * moved[(b - lag) * ROWS : (b - lag + 1) * ROWS]
    out_ref[...] = (feats[0] * jnp.concatenate(blocks, axis=0)).astype(BF16)


def mix(own, got, sent, short_taps, bias, taps, width):
    tokens, chan = own.shape[0], own.shape[1] // 3
    return pl.pallas_call(
        lambda *refs: mix_kernel(width, *refs),
        out_shape=jax.ShapeDtypeStruct((tokens, chan), BF16),
        in_specs=[VMEM] * 6,
        out_specs=VMEM,
        compiler_params=params(8),
        name="mix",
    )(own, got, sent, jnp.transpose(short_taps, (1, 0, 2)), bias, taps)


def out_kernel(*refs, count, owners):
    pieces, (low_ref, high_ref, *acc, out_ref) = refs[:count], refs[count:]
    tokens, chan = out_ref.shape[0], pieces[0].shape[1]
    rows = low_ref.shape[0]
    shards = [ref[i : i + tokens, :] for ref in pieces for i in range(0, ref.shape[0], tokens)]
    for at, w_ref in ((0, low_ref), (rows, high_ref)):
        total = acc[0][:, at : at + rows] if acc else None
        for shard, bits in zip(shards, owners, strict=True):
            owner = lax.axis_index("seq") ^ bits
            span = pl.ds(pl.multiple_of(owner * chan, chan), chan)
            term = contract_last(shard, w_ref[:, span])
            total = term if total is None else total + term
        out_ref[:, at : at + rows] = total


def add_kernel(a_ref, b_ref, out_ref):
    out_ref[...] = (a_ref[...] + b_ref[...]).astype(out_ref.dtype)


def project_out(gated, low, high):
    tokens, rows = gated.shape[0], low.shape[0]
    total = []
    for pieces, owners in gather_groups(gated):
        work = 2 * rows * len(owners) * gated.shape[1]
        total = [
            pl.pallas_call(
                functools.partial(out_kernel, count=len(pieces), owners=owners),
                out_shape=jax.ShapeDtypeStruct((tokens, 2 * rows), F32),
                in_specs=[VMEM] * (len(pieces) + 2 + len(total)),
                out_specs=VMEM,
                compiler_params=params(8),
                cost_estimate=cost(2 * tokens * work, 2 * work),
                name="project_out",
            )(*pieces, low, high, *total)
        ]
    return total[0]


def per_device(tokens_in, norm_gain, in_proj, short_taps, long_taps, skip_bias, out_proj):
    own_tokens, half = tokens_in.shape
    width = 2 * half
    tokens = own_tokens * lax.axis_size("seq")
    chan = in_proj.shape[2] // 2
    weights_out = out_proj.reshape(out_proj.shape[0], -1)
    own, got, sent, taps, loaded = project(
        tokens_in, norm_gain[None, :], in_proj, weights_out, long_taps, tokens
    )
    gated = mix(own, got, sent, short_taps, skip_bias[None, :], taps, width)
    partial_out = project_out(gated, *loaded)
    other = lax.ppermute(partial_out, "mdl", [(0, 1), (1, 0)])
    return pl.pallas_call(
        add_kernel,
        out_shape=jax.ShapeDtypeStruct(other.shape, BF16),
        in_specs=[VMEM] * 2,
        out_specs=VMEM,
        compiler_params=params(4),
        name="add",
    )(partial_out, other)


def per_device_any(tokens_in, norm_gain, in_proj, short_taps, long_taps, skip_bias, out_proj):
    half = tokens_in.shape[1]
    width = 2 * half
    chan = in_proj.shape[2] // 2
    seq_index = lax.axis_index("seq")
    mdl_index = lax.axis_index("mdl")
    values = tokens_in.astype(F32)
    squares = lax.psum(jnp.sum(values * values, axis=1), "mdl")
    scale = lax.rsqrt(squares / width + EPSILON)
    normed = (values * scale[:, None] * norm_gain[None, :]).astype(BF16)
    part = contract_last(
        lax.all_gather(normed, "seq", axis=0, tiled=True), in_proj.reshape(-1, half)
    )
    tokens = part.shape[0]
    part = part.reshape(tokens, 3, 2, chan)
    summed = lax.psum_scatter(part, "mdl", scatter_dimension=2, tiled=True)
    summed = summed.reshape(tokens, 3, chan)
    short_local = lax.dynamic_slice_in_dim(short_taps, mdl_index * chan, chan, 2)
    bias_local = lax.dynamic_slice_in_dim(skip_bias, mdl_index * chan, chan, 0)
    short_count = short_local.shape[0]
    padded = jnp.pad(summed, ((short_count - 1, 0), (0, 0), (0, 0)))
    features = sum(
        short_local[i][None] * padded[short_count - 1 - i : short_count - 1 - i + tokens]
        for i in range(short_count)
    )
    gated = features[:, 1, :] * features[:, 2, :]
    group_width = width // long_taps.shape[0]
    groups = (seq_index * 2 * chan + mdl_index * chan + jnp.arange(chan)) // group_width
    taps = long_taps[groups].T
    reach = min(tokens, taps.shape[0])
    shifted = jnp.pad(gated, ((reach - 1, 0), (0, 0)))
    mixed = bias_local[None, :] * gated + sum(
        taps[i][None, :] * shifted[reach - 1 - i : reach - 1 - i + tokens] for i in range(reach)
    )
    gated_out = (features[:, 0, :] * mixed).astype(BF16)
    rows = out_proj.reshape(out_proj.shape[0], -1)
    folded = contract_last(lax.all_gather(gated_out, "seq", axis=1, tiled=True), rows)
    return lax.psum(folded, "mdl").astype(BF16)


def solution(mesh):
    seq = mesh.shape["seq"]
    in_specs = (
        P(("grp", "seq"), "mdl"),
        P("mdl"),
        P("seq", None, None, "mdl"),
        P(None, None, "seq"),
        P(),
        P("seq"),
        P("seq", "mdl", None),
    )

    def body(tokens_in, norm_gain, in_proj, *others):
        half, chan = tokens_in.shape[1], in_proj.shape[2] // 2
        fits = seq == 8 and mesh.shape["mdl"] == 2
        fits = fits and chan % (PUSH + STREAM) == 0 and half % DEPTH == 0
        path = per_device if fits else per_device_any
        return path(tokens_in, norm_gain, in_proj, *others)

    return jax.shard_map(
        body, mesh=mesh, in_specs=in_specs, out_specs=P("grp", "seq"), check_vma=False
    )
```

```python
import functools

import jax
import jax.numpy as jnp
from jax import lax
from jax.experimental import pallas as pl
from jax.experimental.pallas import tpu as pltpu
from jax.sharding import PartitionSpec as P

EPSILON = 1e-06
F32 = jnp.float32
BF16 = jnp.bfloat16
VMEM = pl.BlockSpec(memory_space=pltpu.VMEM)
ANY = pl.BlockSpec(memory_space=pl.ANY)
MIB = 1 << 20
LANES = 128
ROWS = 8


def contract_last(left, right):
    return lax.dot_general(left, right, (((1,), (1,)), ((), ())), preferred_element_type=F32)


def cost(flops, nbytes):
    return pl.CostEstimate(flops=flops, bytes_accessed=nbytes, transcendentals=0)


def params(mib):
    return pltpu.CompilerParams(vmem_limit_bytes=mib * MIB)


def swap(x, bits):
    count = lax.axis_size("seq")
    return lax.ppermute(x, "seq", [(i, i ^ bits) for i in range(count)])


def stack_kernel(*refs):
    parts = [ref[...].astype(F32) for ref in refs[:-1]]
    refs[-1][...] = jnp.concatenate(parts, axis=0).astype(refs[-1].dtype)


def stack(*parts):
    rows = sum(part.shape[0] for part in parts)
    return pl.pallas_call(
        stack_kernel,
        out_shape=jax.ShapeDtypeStruct((rows,) + parts[0].shape[1:], parts[0].dtype),
        in_specs=[VMEM] * len(parts),
        out_specs=VMEM,
        compiler_params=params(4),
        name="stack",
    )(*parts)


def gather_tokens(x, local):
    pair = stack(local, swap(x, 1))
    return [pair] + [swap(pair, b) for b in (6, 4, 2)], (0, 1, 6, 7, 4, 5, 2, 3)


def gather_groups(x):
    far, mid, close = [swap(x, b) for b in (6, 4, 2)]
    one, two = stack(x, far), stack(mid, close)
    return [([one, two], (0, 6, 4, 2)), ([swap(one, 1)], (1, 7)), ([swap(two, 1)], (5, 3))]


def in_vmem(x):
    return pltpu.with_memory_space_constraint(x, pltpu.VMEM)


def in_hbm(x):
    return pltpu.with_memory_space_constraint(x, pltpu.HBM)


def rows_of(which, chan):
    mine = lax.axis_index("mdl")
    return pl.multiple_of((mine if which == "own" else 1 - mine) * chan, chan)


def prepare_kernel(x_ref, taps_ref, local_ref, spread_ref, group_taps, sem):
    chan = spread_ref.shape[1]
    groups = group_taps.shape[0]
    index = lax.axis_index("seq") * 2 + lax.axis_index("mdl")
    near = pl.ds(pl.multiple_of(index * groups, groups), groups)
    fetch = pltpu.make_async_copy(taps_ref.at[near], group_taps, sem)
    fetch.start()
    local_ref[...] = x_ref[...]
    fetch.wait()
    grp = lax.broadcasted_iota(jnp.int32, (groups, chan), 0)
    ch = lax.broadcasted_iota(jnp.int32, (groups, chan), 1)
    spread = jnp.where(ch // (chan // groups) == grp, 1.0, 0.0)
    spread_ref[...] = lax.dot_general(
        group_taps[...],
        spread,
        (((0,), (0,)), ((), ())),
        preferred_element_type=F32,
        precision=lax.Precision.HIGHEST,
    )[: spread_ref.shape[0]]


def prepare(x, long_taps, tokens, chan):
    reach = min(tokens, long_taps.shape[1])
    groups = long_taps.shape[0] * chan // (2 * x.shape[1])
    return pl.pallas_call(
        prepare_kernel,
        out_shape=(
            jax.ShapeDtypeStruct(x.shape, x.dtype),
            jax.ShapeDtypeStruct((reach, chan), F32),
        ),
        in_specs=[VMEM, ANY],
        out_specs=(VMEM,) * 2,
        scratch_shapes=[
            pltpu.VMEM((groups, long_taps.shape[1]), F32),
            pltpu.SemaphoreType.DMA,
        ],
        compiler_params=params(4),
        cost_estimate=cost(12 * 10**9, 4 * MIB),
        name="prepare",
    )(x, in_hbm(long_taps))


def place_rows(pieces, owners, out_ref):
    per = out_ref.shape[1]
    shards = [
        piece[...].astype(F32)[i : i + per]
        for piece in pieces
        for i in range(0, piece.shape[0], per)
    ]
    for shard, bits in zip(shards, owners, strict=True):
        out_ref[lax.axis_index("seq") ^ bits] = shard


PUSH = 128
STREAM = 128
DEPTH = 512


def channel_sums(xg_ref, xt_ref, w_ref, which, out_ref, chan):
    tokens, half = xg_ref.shape
    first = rows_of(which, chan)
    for p in range(3):
        for at in range(0, chan, PUSH + STREAM):
            low = pl.ds(pl.multiple_of(first + at, PUSH), PUSH)
            high = pl.ds(pl.multiple_of(first + at + PUSH, STREAM), STREAM)
            pushed = streamed = None
            for depth in range(0, half, DEPTH):
                cut = slice(depth, depth + DEPTH)
                term = contract_last(xg_ref[:, cut], w_ref[0, p, low, cut])
                pushed = term if pushed is None else pushed + term
                term = jnp.dot(w_ref[0, p, high, cut], xt_ref[cut, :], preferred_element_type=F32)
                streamed = term if streamed is None else streamed + term
            to = p * chan + at
            out_ref[:, to : to + PUSH] = pushed
            out_ref[:, to + PUSH : to + PUSH + STREAM] = streamed.T


def partner_kernel(*refs, owners):
    pieces, refs = refs[:-9], refs[-9:]
    gain_ref, w_ref, wo_ref, out_ref, xg_ref, xt_ref, load_ref, raw_ref, sem = refs
    load = pltpu.make_async_copy(wo_ref.at[pl.ds(0, load_ref.shape[0])], load_ref, sem)
    load.start()
    tokens = out_ref.shape[0]
    place_rows(pieces, owners, raw_ref)
    values = jnp.concatenate([raw_ref[i] for i in range(raw_ref.shape[0])], axis=0)
    squares = jnp.sum(values * values, axis=1, keepdims=True)
    out_ref[:, -LANES:] = jnp.broadcast_to(squares, (tokens, LANES))
    gained = (values * gain_ref[...]).astype(BF16)
    xg_ref[...] = gained
    xt_ref[...] = gained.astype(F32).T.astype(BF16)
    channel_sums(xg_ref, xt_ref, w_ref, "partner", out_ref, w_ref.shape[2] // 2)
    load.wait()


def own_kernel(xg_ref, xt_ref, w_ref, wo_ref, out_ref, load_ref, sem):
    rows = load_ref.shape[0]
    load = pltpu.make_async_copy(wo_ref.at[pl.ds(wo_ref.shape[0] - rows, rows)], load_ref, sem)
    load.start()
    channel_sums(xg_ref, xt_ref, w_ref, "own", out_ref, w_ref.shape[2] // 2)
    load.wait()


def project(tokens_in, gain, weights, weights_out, long_taps, tokens):
    chan = weights.shape[2] // 2
    half = weights.shape[3]
    local, taps = prepare(tokens_in, long_taps, tokens, chan)
    pieces, owners = gather_tokens(tokens_in, local)
    work = cost(2 * tokens * chan * half * 3, weights.size)
    rows = weights_out.shape[0] // 2
    half_out = pltpu.VMEM((rows, weights_out.shape[1]), weights_out.dtype)
    weights_out = in_hbm(weights_out)
    partner, xg, xt, low = pl.pallas_call(
        functools.partial(partner_kernel, owners=owners),
        out_shape=(
            jax.ShapeDtypeStruct((tokens, 3 * chan + LANES), F32),
            jax.ShapeDtypeStruct((tokens, half), BF16),
            jax.ShapeDtypeStruct((half, tokens), BF16),
            half_out,
        ),
        in_specs=[VMEM] * (2 + len(pieces)) + [ANY],
        out_specs=(VMEM,) * 4,
        scratch_shapes=[
            pltpu.VMEM((len(owners), tokens // len(owners), half), F32),
            pltpu.SemaphoreType.DMA,
        ],
        compiler_params=params(8),
        cost_estimate=work,
        name="project_partner",
    )(*pieces, gain, weights, weights_out)
    got = lax.ppermute(partner, "mdl", [(0, 1), (1, 0)])
    own, high = pl.pallas_call(
        own_kernel,
        out_shape=(
            jax.ShapeDtypeStruct((tokens, 3 * chan), F32),
            half_out,
        ),
        in_specs=[VMEM] * 3 + [ANY],
        out_specs=(VMEM,) * 2,
        scratch_shapes=[pltpu.SemaphoreType.DMA],
        compiler_params=params(8),
        cost_estimate=work,
        name="project_own",
    )(xg, xt, weights, weights_out)
    return own, got, partner, taps, (in_vmem(low), in_vmem(high))


def delay(x, rows):
    if rows == 0:
        return x
    index = lax.broadcasted_iota(jnp.int32, x.shape, 0)
    return jnp.where(index >= rows, pltpu.roll(x, rows, axis=0), 0.0)


def mix_kernel(width, own_ref, got_ref, sent_ref, short_ref, bias_ref, taps_ref, out_ref):
    tokens, chan = out_ref.shape
    reach = taps_ref.shape[0]
    first = pl.multiple_of(lax.axis_index("mdl") * chan, chan)
    squares = sent_ref[:, 3 * chan : 3 * chan + 1] + got_ref[:, 3 * chan : 3 * chan + 1]
    scale = lax.rsqrt(squares / width + EPSILON)
    feats = []
    for branch in range(3):
        span = slice(branch * chan, (branch + 1) * chan)
        total = (own_ref[:, span] + got_ref[:, span]) * scale
        feat = None
        for offset in range(short_ref.shape[1]):
            term = short_ref[branch, pl.ds(offset, 1), pl.ds(first, chan)] * delay(total, offset)
            feat = term if feat is None else feat + term
        feats.append(feat)
    gated = feats[1] * feats[2]
    mixed = bias_ref[:, pl.ds(first, chan)] * gated
    blocks = [mixed[b * ROWS : (b + 1) * ROWS] for b in range(tokens // ROWS)]
    for shift in range(ROWS):
        moved = delay(gated, shift)
        for lag in range(reach // ROWS):
            tap = taps_ref[pl.ds(lag * ROWS + shift, 1), :]
            for b in range(lag, tokens // ROWS):
                blocks[b] = blocks[b] + tap * moved[(b - lag) * ROWS : (b - lag + 1) * ROWS]
    out_ref[...] = (feats[0] * jnp.concatenate(blocks, axis=0)).astype(BF16)


def mix(own, got, sent, short_taps, bias, taps, width):
    tokens, chan = own.shape[0], own.shape[1] // 3
    return pl.pallas_call(
        lambda *refs: mix_kernel(width, *refs),
        out_shape=jax.ShapeDtypeStruct((tokens, chan), BF16),
        in_specs=[VMEM] * 6,
        out_specs=VMEM,
        compiler_params=params(8),
        name="mix",
    )(own, got, sent, jnp.transpose(short_taps, (1, 0, 2)), bias, taps)


def out_kernel(*refs, count, owners):
    pieces, (low_ref, high_ref, *acc, out_ref) = refs[:count], refs[count:]
    tokens, chan = out_ref.shape[0], pieces[0].shape[1]
    rows = low_ref.shape[0]
    shards = [ref[i : i + tokens, :] for ref in pieces for i in range(0, ref.shape[0], tokens)]
    for at, w_ref in ((0, low_ref), (rows, high_ref)):
        total = acc[0][:, at : at + rows] if acc else None
        for shard, bits in zip(shards, owners, strict=True):
            owner = lax.axis_index("seq") ^ bits
            span = pl.ds(pl.multiple_of(owner * chan, chan), chan)
            term = contract_last(shard, w_ref[:, span])
            total = term if total is None else total + term
        out_ref[:, at : at + rows] = total


def add_kernel(a_ref, b_ref, out_ref):
    out_ref[...] = (a_ref[...] + b_ref[...]).astype(out_ref.dtype)


def project_out(gated, low, high):
    tokens, rows = gated.shape[0], low.shape[0]
    total = []
    for pieces, owners in gather_groups(gated):
        work = 2 * rows * len(owners) * gated.shape[1]
        total = [
            pl.pallas_call(
                functools.partial(out_kernel, count=len(pieces), owners=owners),
                out_shape=jax.ShapeDtypeStruct((tokens, 2 * rows), F32),
                in_specs=[VMEM] * (len(pieces) + 2 + len(total)),
                out_specs=VMEM,
                compiler_params=params(8),
                cost_estimate=cost(2 * tokens * work, 2 * work),
                name="project_out",
            )(*pieces, low, high, *total)
        ]
    return total[0]


def per_device(tokens_in, norm_gain, in_proj, short_taps, long_taps, skip_bias, out_proj):
    own_tokens, half = tokens_in.shape
    width = 2 * half
    tokens = own_tokens * lax.axis_size("seq")
    chan = in_proj.shape[2] // 2
    weights_out = out_proj.reshape(out_proj.shape[0], -1)
    own, got, sent, taps, loaded = project(
        tokens_in, norm_gain[None, :], in_proj, weights_out, long_taps, tokens
    )
    gated = mix(own, got, sent, short_taps, skip_bias[None, :], taps, width)
    partial_out = project_out(gated, *loaded)
    other = lax.ppermute(partial_out, "mdl", [(0, 1), (1, 0)])
    return pl.pallas_call(
        add_kernel,
        out_shape=jax.ShapeDtypeStruct(other.shape, BF16),
        in_specs=[VMEM] * 2,
        out_specs=VMEM,
        compiler_params=params(4),
        name="add",
    )(partial_out, other)


def per_device_any(tokens_in, norm_gain, in_proj, short_taps, long_taps, skip_bias, out_proj):
    half = tokens_in.shape[1]
    width = 2 * half
    chan = in_proj.shape[2] // 2
    seq_index = lax.axis_index("seq")
    mdl_index = lax.axis_index("mdl")
    values = tokens_in.astype(F32)
    squares = lax.psum(jnp.sum(values * values, axis=1), "mdl")
    scale = lax.rsqrt(squares / width + EPSILON)
    normed = (values * scale[:, None] * norm_gain[None, :]).astype(BF16)
    part = contract_last(
        lax.all_gather(normed, "seq", axis=0, tiled=True), in_proj.reshape(-1, half)
    )
    tokens = part.shape[0]
    part = part.reshape(tokens, 3, 2, chan)
    summed = lax.psum_scatter(part, "mdl", scatter_dimension=2, tiled=True)
    summed = summed.reshape(tokens, 3, chan)
    short_local = lax.dynamic_slice_in_dim(short_taps, mdl_index * chan, chan, 2)
    bias_local = lax.dynamic_slice_in_dim(skip_bias, mdl_index * chan, chan, 0)
    short_count = short_local.shape[0]
    padded = jnp.pad(summed, ((short_count - 1, 0), (0, 0), (0, 0)))
    features = sum(
        short_local[i][None] * padded[short_count - 1 - i : short_count - 1 - i + tokens]
        for i in range(short_count)
    )
    gated = features[:, 1, :] * features[:, 2, :]
    group_width = width // long_taps.shape[0]
    groups = (seq_index * 2 * chan + mdl_index * chan + jnp.arange(chan)) // group_width
    taps = long_taps[groups].T
    reach = min(tokens, taps.shape[0])
    shifted = jnp.pad(gated, ((reach - 1, 0), (0, 0)))
    mixed = bias_local[None, :] * gated + sum(
        taps[i][None, :] * shifted[reach - 1 - i : reach - 1 - i + tokens] for i in range(reach)
    )
    gated_out = (features[:, 0, :] * mixed).astype(BF16)
    rows = out_proj.reshape(out_proj.shape[0], -1)
    folded = contract_last(lax.all_gather(gated_out, "seq", axis=1, tiled=True), rows)
    return lax.psum(folded, "mdl").astype(BF16)


def solution(mesh):
    seq = mesh.shape["seq"]
    in_specs = (
        P(("grp", "seq"), "mdl"),
        P("mdl"),
        P("seq", None, None, "mdl"),
        P(None, None, "seq"),
        P(),
        P("seq"),
        P("seq", "mdl", None),
    )

    def body(tokens_in, norm_gain, in_proj, *others):
        half, chan = tokens_in.shape[1], in_proj.shape[2] // 2
        fits = seq == 8 and mesh.shape["mdl"] == 2
        fits = fits and chan % (PUSH + STREAM) == 0 and half % DEPTH == 0
        path = per_device if fits else per_device_any
        return path(tokens_in, norm_gain, in_proj, *others)

    return jax.shard_map(
        body, mesh=mesh, in_specs=in_specs, out_specs=P("grp", "seq"), check_vma=False
    )
```
